768 devices in a mesh: group: 16 (over y, core), dom: 48 (over x, z).
Axes of the slice: x: 4, y: 8, z: 12, core: 2. Of those that a mesh axis runs over, the one named last changes fastest.
Arguments:
- features: bfloat16 [196608, 512], P(('group', 'dom')), may hold values from -6 to 6
- cotangent: bfloat16 [196608, 512], P(('group', 'dom')), may hold values from -6 to 6
- w_self: bfloat16 [512, 512], replicated, may hold values from -0.25 to 0.25
- w_neigh: bfloat16 [512, 512], replicated, may hold values from -0.5 to 0.5
- bias: float32 [512], replicated, may hold values from -3 to 3
- neighbours: int32 [196608, 10], P(('group', 'dom')), may hold values from 0 to 3327, as said below
- send_rows: int32 [768, 48, 32], P(('group', 'dom')), may hold values from -1 to 255, as said below
- hub_local: int32 [1536], P(('group', 'dom')), may hold values from 0 to 255, as said below
Outputs:
- output: bfloat16 [196608, 512], P(('group', 'dom'))
- grad_features: float32 [196608, 512], P(('group', 'dom'))
The draws below stay inside these ranges and needn't reach their ends.
Inputs may be any that keep to these rules, and one draw needn't show every extreme that they name: `send_rows`: row i, peer p: the distinct local rows of device i sent to device p of its group fill the first slots, the rest are -1; a device sends nothing to itself; in every group some device receives 32 rows from each other device of the group, and loads differ widely between receivers. `neighbours`: positions below 256 are own rows; positions 256 + p * 32 + s address only filled slots; positions from 1792 on are hubs, a few hubs far more often than others. `hub_local`: the 2 entries of one device are distinct.
All inputs are finite; a program needn't handle non-finite values.
Results may differ from the reference program's by a relative error of at most 0.0039.
Values may be sent and summed in bfloat16 or wider, within the bound.
A program may use at most 32 MiB of HBM per device.

```python
import jax
import jax.numpy as jnp
from jax import lax

WIDTH = 512
VERT_DEV = 256
BLOCK_ROWS = 32
FANOUT = 10
HUB_DEV = 2
HUBS = 1536
TABLE = 3328
VERTICES = 196608
N_GROUP = 16
N_DOM = 48


def pair_counts(key):
    key = jax.random.fold_in(key, 101)
    key_shift, key_warm, key_cold = jax.random.split(key, 3)
    shift = jax.random.randint(key_shift, (N_GROUP, 1, 1), 0, 8)
    sender = jnp.arange(N_DOM)[None, :, None]
    target = jnp.arange(N_DOM)[None, None, :]
    warm = (target + shift) % 4 == 0
    filled = (target + shift) % 8 == 0
    warm_count = jax.random.randint(key_warm, (N_GROUP, N_DOM, N_DOM), BLOCK_ROWS // 2, BLOCK_ROWS + 1)
    cold_count = jax.random.randint(key_cold, (N_GROUP, N_DOM, N_DOM), 1, BLOCK_ROWS // 4 + 2)
    counts = jnp.where(filled, BLOCK_ROWS, jnp.where(warm, warm_count, cold_count))
    counts = jnp.where(sender == target, 0, counts)
    return counts.astype(jnp.int32)


def draw_send_rows(key, part):
    counts = pair_counts(key).reshape(N_GROUP * N_DOM, N_DOM)
    key = jax.random.fold_in(key, 7)
    keys = jax.random.split(key, N_GROUP * N_DOM * N_DOM)
    orders = jax.vmap(lambda one: jax.random.permutation(one, VERT_DEV)[:BLOCK_ROWS])(keys)
    orders = orders.reshape(N_GROUP * N_DOM, N_DOM, BLOCK_ROWS).astype(jnp.int32)
    slots = jnp.arange(BLOCK_ROWS, dtype=jnp.int32)[None, None, :]
    return jnp.where(slots < counts[:, :, None], orders, -1).astype(jnp.int32)


def draw_neighbours(key, part):
    counts = pair_counts(key)
    devices = N_GROUP * N_DOM
    received = counts.transpose(0, 2, 1).reshape(devices, N_DOM)
    running = jnp.cumsum(received, axis=1).astype(jnp.int32)
    starts = running - received
    totals = running[:, -1]
    key = jax.random.fold_in(key, 11)
    key_kind, key_own, key_pick, key_top, key_hub, key_perm = jax.random.split(key, 6)
    shape = (devices, VERT_DEV * FANOUT)
    kind = jax.random.randint(key_kind, shape, 0, 10)
    own = jax.random.randint(key_own, shape, 0, VERT_DEV)
    picked = jax.random.randint(key_pick, shape, 0, totals[:, None])
    sender = jax.vmap(lambda run, val: jnp.searchsorted(run, val, side='right'))(running, picked).astype(jnp.int32)
    offset = picked - jnp.take_along_axis(starts, sender, axis=1)
    border = VERT_DEV + sender * BLOCK_ROWS + offset
    tops = jax.random.randint(key_top, shape, 1, HUBS + 1)
    lowest = jax.random.randint(key_hub, shape, 0, tops)
    hub_order = jax.random.permutation(key_perm, HUBS).astype(jnp.int32)
    hub_pos = VERT_DEV + N_DOM * BLOCK_ROWS + hub_order[lowest]
    chosen = jnp.where(kind < 4, own, jnp.where(kind < 7, border, hub_pos))
    return chosen.reshape(devices * VERT_DEV, FANOUT).astype(jnp.int32)


def draw_hub_local(key, part):
    key = jax.random.fold_in(key, 23)
    keys = jax.random.split(key, N_GROUP * N_DOM)
    picks = jax.vmap(lambda one: jax.random.permutation(one, VERT_DEV)[:HUB_DEV])(keys)
    return picks.reshape(HUBS).astype(jnp.int32)


def block_scale(stream_key, extent, shards, least, top_value):
    def one(dim, shards_of):
        steps = jax.random.uniform(jax.random.fold_in(jax.random.fold_in(stream_key, 6), dim), (shards_of,), jnp.float32, least / len(shards), top_value / len(shards))
        return jnp.repeat(jnp.exp(steps), extent[dim] // shards_of).reshape((-1,) + (1,) * (len(extent) - dim - 1))

    level = one(*shards[0])
    for cut in shards[1:]:
        level = level * one(*cut)
    return level


def normal_values(key, shape, width, limit, pieces=(), kind=jnp.bfloat16):
    factor_of = block_scale(key, shape, pieces, -0.22, 0.18) if pieces else 1.0
    result = jax.random.normal(key, shape, jnp.float32) * width * factor_of
    return jnp.minimum(jnp.maximum(result, -limit), limit).astype(kind)


def setup_inputs(seed: int = 0) -> dict:
    splits = jax.random.split(jax.random.key(seed), 9)
    return {
        "features": normal_values(splits[0], (VERTICES, WIDTH), 1.0, 6.0, ((0, 768),)),
        "cotangent": normal_values(splits[1], (VERTICES, WIDTH), 1.0, 6.0, ((0, 768),)),
        "w_self": normal_values(splits[2], (WIDTH, WIDTH), WIDTH ** -0.5, 0.25),
        "w_neigh": normal_values(splits[3], (WIDTH, WIDTH), (WIDTH // 4) ** -0.5, 0.5),
        "bias": normal_values(splits[4], (WIDTH,), 0.5, 3.0, (), jnp.float32),
        "neighbours": draw_neighbours(jax.random.fold_in(splits[8], 71), 0),
        "send_rows": draw_send_rows(jax.random.fold_in(splits[8], 71), 0),
        "hub_local": draw_hub_local(jax.random.fold_in(splits[8], 71), 0),
    }


def reference(features, cotangent, w_self, w_neigh, bias, neighbours, send_rows, hub_local):
    devices = N_GROUP * N_DOM
    device_ids = jnp.arange(devices, dtype=jnp.int32)
    own_ids = device_ids[:, None] * VERT_DEV + jnp.arange(VERT_DEV, dtype=jnp.int32)[None, :]
    sent = send_rows.reshape(N_GROUP, N_DOM, N_DOM, BLOCK_ROWS).transpose(0, 2, 1, 3)
    sender_dev = jnp.arange(N_GROUP, dtype=jnp.int32)[:, None] * N_DOM + jnp.arange(N_DOM, dtype=jnp.int32)[None, :]
    border_ids = sender_dev[:, None, :, None] * VERT_DEV + jnp.maximum(sent, 0)
    border_ids = border_ids.reshape(devices, N_DOM * BLOCK_ROWS).astype(jnp.int32)
    hub_ids = (jnp.arange(HUBS, dtype=jnp.int32) // HUB_DEV) * VERT_DEV + hub_local
    table_ids = jnp.concatenate([own_ids, border_ids, jnp.broadcast_to(hub_ids[None, :], (devices, HUBS))], axis=1).astype(jnp.int32)
    local_pos = neighbours.reshape(devices, VERT_DEV * FANOUT)
    global_nbr = jnp.take_along_axis(table_ids, local_pos, axis=1).reshape(VERTICES, FANOUT)
    agg_sum = jnp.zeros((VERTICES, WIDTH), jnp.float32)
    for column in range(FANOUT):
        agg_sum = agg_sum + features[global_nbr[:, column]].astype(jnp.float32)
    mean_rows = (agg_sum / FANOUT).astype(jnp.bfloat16)
    pre = jnp.dot(features, w_self, preferred_element_type=jnp.float32)
    pre = pre + jnp.dot(mean_rows, w_neigh, preferred_element_type=jnp.float32) + bias.astype(jnp.float32)
    output = jax.nn.silu(pre).astype(jnp.bfloat16)
    sigm = jax.nn.sigmoid(pre)
    grad_pre = (cotangent.astype(jnp.float32) * sigm * (1.0 + pre * (1.0 - sigm))).astype(jnp.bfloat16)
    grad_self = jnp.dot(grad_pre, w_self.T, preferred_element_type=jnp.float32)
    grad_mean = (jnp.dot(grad_pre, w_neigh.T, preferred_element_type=jnp.float32) / FANOUT).astype(jnp.bfloat16)
    positions = jnp.arange(TABLE, dtype=jnp.int32)
    border_mask = (positions >= VERT_DEV) & (positions < VERT_DEV + N_DOM * BLOCK_ROWS)

    def visit(total, item):
        grad_rows, position, row_ids = item
        terms = jnp.broadcast_to(grad_rows.astype(jnp.float32)[:, None, :], (VERT_DEV, FANOUT, WIDTH)).reshape(VERT_DEV * FANOUT, WIDTH)
        slots = jnp.zeros((TABLE, WIDTH), jnp.float32).at[position.reshape(-1)].add(terms)
        rounded = lax.optimization_barrier(slots.astype(jnp.bfloat16)).astype(jnp.float32)
        slots = jnp.where(border_mask[:, None], rounded, slots)
        return total.at[row_ids].add(slots), None

    total, unused = lax.scan(visit, jnp.zeros((VERTICES, WIDTH), jnp.float32),
                             (grad_mean.reshape(devices, VERT_DEV, WIDTH), neighbours.reshape(devices, VERT_DEV, FANOUT), table_ids))
    return output, grad_self + total
```

```python
import functools

import jax
import jax.numpy as jnp
from jax import lax
from jax.experimental import pallas as pl
from jax.experimental.pallas import tpu as pltpu
from jax.sharding import PartitionSpec as P

ZN = 12
F32 = jnp.float32
BF16 = jnp.bfloat16


def dot_t(left, right):
    return lax.dot_general(left, right, (((0,), (0,)), ((), ())), preferred_element_type=F32)


def dot_b(left, right):
    return lax.dot_general(left, right, (((1,), (1,)), ((), ())), preferred_element_type=F32)


def dot(left, right):
    return jnp.dot(left, right, preferred_element_type=F32)


def kernel(
    yn, xn, zn, feat, cot, ws, wn, bias, nbrt, lst, hubl, out, gout,
    tab, sel, orow, arr, grow, ret, hubtab,
    ha_s, ha, hb_s, hb, hubg, sib, ysr, yrr, ysl, yrl, xb_s, xb, za_s, za,
    sem_a2a, sem_ha, sem_hb, sem_yr, sem_yl, sem_sib, sem_sibg, sem_gr, sem_gl, sem_xb, sem_za,
):
    verts, width = feat.shape
    fanout = nbrt.shape[0]
    peers, slots = arr.shape[0], arr.shape[1]
    lanes = 128
    quarter = width // lanes
    near = peers * slots
    group = lax.axis_index("group")
    dom = lax.axis_index("dom")
    y, core = group // 2, lax.rem(group, 2)
    x, z = dom // zn, lax.rem(dom, zn)
    half_y = yn // 2

    def up(step):
        return lax.rem(y + step + 2 * yn, yn)

    def copy(src, dst, sems, at, **to):
        return pltpu.make_async_remote_copy(
            src_ref=src, dst_ref=dst, send_sem=sems.at[(0,) + at], recv_sem=sems.at[(1,) + at],
            device_id=to, device_id_type=pl.DeviceIdType.MESH,
        )

    right = {"group": up(1) * 2 + core}
    left = {"group": up(-1) * 2 + core}
    sibling = {"group": y * 2 + 1 - core}

    barrier = pltpu.get_barrier_semaphore()

    def greet(i, carry):
        pl.semaphore_signal(barrier, 1, device_id={"dom": lax.rem(dom + i, peers)}, device_id_type=pl.DeviceIdType.MESH)
        return carry

    lax.fori_loop(1, peers, greet, 0)
    for partner in (right, left, sibling):
        pl.semaphore_signal(barrier, 1, device_id=partner, device_id_type=pl.DeviceIdType.MESH)

    row_id = lax.broadcasted_iota(jnp.int32, (16, verts), 0)
    vert_id = lax.broadcasted_iota(jnp.int32, (16, verts), 1)
    hub0, hub1 = hubl[0], hubl[1]
    wanted = jnp.where(row_id == 0, hub0, jnp.where(row_id == 1, hub1, -1))
    hub_rows = dot((vert_id == wanted).astype(BF16), feat[...])
    for q in range(quarter):
        ha_s[2 * q:2 * q + 2, :] = hub_rows[0:2, q * lanes:(q + 1) * lanes]
    ha[z] = ha_s[...]

    pl.semaphore_wait(barrier, peers + 2)

    def send_ha(i):
        to = lax.rem(z + i, zn)
        return copy(ha_s, ha.at[z], sem_ha, (i,), dom=x * zn + to)

    def loop(lo, hi, body):
        lax.fori_loop(lo, hi, lambda i, c: (body(i), c)[1], 0)

    loop(1, zn, lambda i: send_ha(i).start())

    chunks = lst.shape[0]
    per = peers // chunks
    sub_id = lax.broadcasted_iota(jnp.int32, (verts, lanes), 0)

    def pick(c):
        chosen = (sub_id == lst[pl.ds(c, 1), :]).astype(BF16)
        sel[c] = chosen
        rows = dot_t(chosen, feat[...]).astype(BF16)
        orow[pl.ds(c * per, per)] = rows.reshape(per, slots, width)

    loop(0, chunks, pick)
    arr[dom] = jnp.zeros((slots, width), BF16)
    ret[dom] = jnp.zeros((slots, width), BF16)

    def all_to_all(src, dst, way):
        def send(i):
            to = lax.rem(dom + 7 * i, peers)
            copy(src.at[to], dst.at[dom], sem_a2a, (way,), dom=to).start()

        loop(1, peers, send)

    def all_to_all_wait(src, dst, way):
        some = pl.ds(0, peers - 1)
        done = pltpu.make_async_remote_copy(
            src_ref=src.at[some], dst_ref=dst.at[some], send_sem=sem_a2a.at[0, way], recv_sem=sem_a2a.at[1, way],
            device_id={"dom": lax.rem(dom + 1, peers)}, device_id_type=pl.DeviceIdType.MESH,
        )
        done.wait()

    all_to_all(orow, arr, 0)

    loop(1, zn, lambda i: send_ha(i).wait())
    for zz in range(zn):
        for q in range(quarter):
            hb_s[2 * zz:2 * zz + 2, q * lanes:(q + 1) * lanes] = ha[zz, 2 * q:2 * q + 2, :]
    hb[x] = hb_s[...]

    def send_hb(i):
        return copy(hb_s, hb.at[x], sem_hb, (i,), dom=lax.rem(x + i, xn) * zn + z)

    for i in range(1, xn):
        send_hb(i).start()

    tall = 128

    def tally(i):
        rows = lax.broadcasted_iota(jnp.int32, (tall, verts), 0) + i * tall
        total = jnp.zeros((tall, verts), F32)
        for e in range(fanout):
            total = jnp.where(nbrt[e:e + 1, :] == rows, total + 1.0, total)
        tab[pl.ds(pl.multiple_of(i * tall, tall), tall), :] = total.astype(BF16)

    tiles = tab.shape[0] // tall
    cuts = [tiles * k // (half_y + 2) for k in range(half_y + 3)]
    loop(cuts[0], cuts[1], tally)

    for i in range(1, xn):
        send_hb(i).wait()
    block = hubtab.shape[1]
    hubtab[group] = hb[...].reshape(block, width).astype(BF16)

    def send_y(way, step):
        sems, owner, to = (sem_yr, up(1 - step), right) if way > 0 else (sem_yl, up(step - 1), left)
        part = hubtab.at[owner * 2 + core]
        if step == half_y:
            part = part.at[pl.ds(0 if way > 0 else block // 2, block // 2)]
        return copy(part, part, sems, (step,), **to)

    def send_sib(at, owner_y):
        part = hubtab.at[owner_y * 2 + core]
        return copy(part, part, sem_sib, (at,), **sibling)

    send_sib(0, y).start()
    send_y(1, 1).start()
    send_y(-1, 1).start()
    for step in range(1, half_y + 1):
        loop(cuts[step], cuts[step + 1], tally)
        send_y(1, step).wait_recv()
        send_y(-1, step).wait_recv()
        if step < half_y:
            send_y(1, step + 1).start()
            send_y(-1, step + 1).start()
            send_sib(2 * step - 1, up(-step)).start()
            send_sib(2 * step, up(step)).start()
        else:
            send_sib(2 * step - 1, up(step)).start()
    loop(cuts[half_y + 1], cuts[half_y + 2], tally)
    for step in range(1, half_y + 1):
        send_y(1, step).wait_send()
        send_y(-1, step).wait_send()

    hub_at = verts + near
    agg = dot_t(tab[0:verts, :], feat[...])
    pre = dot(feat[...], ws[...]) + bias[...]
    for i in range(yn):
        send_sib(i, y).wait()
    agg += dot_t(tab[hub_at:, :], hubtab[...].reshape(2 * yn * block, width))
    all_to_all_wait(orow, arr, 0)
    agg += dot_t(tab[verts:hub_at, :], arr[...].reshape(near, width))

    mean = (agg / fanout).astype(BF16)
    pre += dot(mean, wn[...])
    sigm = jax.nn.sigmoid(pre)
    out[...] = (pre * sigm).astype(BF16)
    grad_pre = (cot[...].astype(F32) * sigm * (1.0 + pre * (1.0 - sigm))).astype(BF16)
    grad_mean = (dot_b(grad_pre, wn[...]) / fanout).astype(BF16)

    grow[...] = dot(tab[verts:hub_at, :], grad_mean).astype(BF16).reshape(peers, slots, width)
    all_to_all(grow, ret, 1)

    hubg[...] = dot(tab[hub_at:, :], grad_mean).reshape(2 * yn, block, width)

    def send_sibg(i):
        owner = up(i)
        return copy(hubg.at[owner * 2 + 1 - core], sib.at[owner], sem_sibg, (i,), **sibling)

    order = [half_y]
    for i in range(half_y - 1, 0, -1):
        order += [i, yn - i]
    order += [0]
    for i in order:
        send_sibg(i).start()
    gout[...] = dot(tab[0:verts, :], grad_mean) + dot_b(grad_pre, ws[...])

    def mine(step):
        owner = up(step)
        return hubg[owner * 2 + core] + sib[owner]

    def send_g(way, k):
        sems, src, dst, to = (sem_gr, ysr, yrr, right) if way > 0 else (sem_gl, ysl, yrl, left)
        src, dst = src.at[k], dst.at[k]
        if k == half_y:
            part = pl.ds(0 if way > 0 else block // 2, block // 2)
            src, dst = src.at[part], dst.at[part]
        return copy(src, dst, sems, (k,), **to)

    lower, upper = slice(0, block // 2), slice(block // 2, block)
    send_sibg(half_y).wait_recv()
    far = mine(half_y)
    ysr[half_y, lower] = far[lower]
    ysl[half_y, upper] = far[upper]
    send_g(1, half_y).start()
    send_g(-1, half_y).start()
    for k in range(half_y - 1, -1, -1):
        for i in sorted({k, (yn - k) % yn}):
            send_sibg(i).wait_recv()
        send_g(1, k + 1).wait_recv()
        send_g(-1, k + 1).wait_recv()
        if k == half_y - 1:
            if k > 0:
                on_r, on_l = mine(k), mine(-k)
                ysr[k, lower] = on_r[lower] + yrr[k + 1, lower]
                ysr[k, upper] = on_r[upper]
                ysl[k, lower] = on_l[lower]
                ysl[k, upper] = on_l[upper] + yrl[k + 1, upper]
            else:
                total = mine(0)
                ysr[0, lower] = total[lower] + yrr[1, lower]
                ysr[0, upper] = total[upper] + yrl[1, upper]
        elif k > 0:
            ysr[k] = mine(k) + yrr[k + 1]
            ysl[k] = mine(-k) + yrl[k + 1]
        else:
            ysr[0] = mine(0) + yrr[1] + yrl[1]
        if k > 0:
            send_g(1, k).start()
            send_g(-1, k).start()
    xb_s[...] = ysr[0].reshape(xn, 2 * zn, width)

    def send_xb(i):
        to = lax.rem(x + i, xn)
        return copy(xb_s.at[to], xb.at[i], sem_xb, (i,), dom=to * zn + z)

    for i in range(1, xn):
        send_xb(i).start()
    total = xb_s[x]
    for i in range(1, xn):
        send_xb(i).wait_recv()
        total = total + xb[i]
    for zz in range(zn):
        for q in range(quarter):
            za_s[zz, 2 * q:2 * q + 2, :] = total[2 * zz:2 * zz + 2, q * lanes:(q + 1) * lanes]

    def send_za(i):
        to = lax.rem(z + i, zn)
        return copy(za_s.at[to], za.at[i], sem_za, (i,), dom=x * zn + to)

    loop(1, zn, lambda i: send_za(i).start())
    all_to_all_wait(grow, ret, 1)

    def back(c):
        rows = ret[pl.ds(c * per, per)].reshape(lanes, width)
        gout[...] += dot(sel[c], rows)

    loop(0, chunks, back)
    loop(1, zn, lambda i: send_za(i).wait_recv())
    za[0] = za_s[z]
    hub_sum = za[0]
    for i in range(1, zn):
        hub_sum = hub_sum + za[i]
    rows_of = lax.broadcasted_iota(jnp.int32, (verts, lanes), 0)
    for q in range(quarter):
        cols = slice(q * lanes, (q + 1) * lanes)
        gout[:, cols] += jnp.where(rows_of == hub0, hub_sum[2 * q:2 * q + 1], 0.0) + jnp.where(
            rows_of == hub1, hub_sum[2 * q + 1:2 * q + 2], 0.0
        )

    for i in range(yn):
        send_sibg(i).wait_send()
    for k in range(1, half_y + 1):
        send_g(1, k).wait_send()
        send_g(-1, k).wait_send()
    for i in range(1, xn):
        send_xb(i).wait_send()
    loop(1, zn, lambda i: send_za(i).wait_send())


def body(features, cotangent, w_self, w_neigh, bias, neighbours, send_rows, hub_local):
    verts, width = features.shape
    peers, slots = send_rows.shape[1:]
    xn, zn = peers // ZN, ZN
    groups = lax.axis_size("group")
    yn = groups // 2
    half_y = yn // 2
    near = peers * slots
    block = 2 * peers
    lst = send_rows.reshape(near // 128, 128)
    vmem = pl.BlockSpec(memory_space=pltpu.VMEM)
    dma = pltpu.SemaphoreType.DMA
    return pl.pallas_call(
        functools.partial(kernel, yn, xn, zn),
        out_shape=(
            jax.ShapeDtypeStruct((verts, width), BF16),
            jax.ShapeDtypeStruct((verts, width), F32),
        ),
        in_specs=[vmem] * 7 + [pl.BlockSpec(memory_space=pltpu.SMEM)],
        out_specs=(vmem, vmem),
        scratch_shapes=[
            pltpu.VMEM((verts + near + groups * block, verts), BF16),
            pltpu.VMEM((near // 128, verts, 128), BF16),
            pltpu.VMEM((peers, slots, width), BF16),
            pltpu.VMEM((peers, slots, width), BF16),
            pltpu.VMEM((peers, slots, width), BF16),
            pltpu.VMEM((peers, slots, width), BF16),
            pltpu.VMEM((groups, block, width), BF16),
            pltpu.VMEM((width // 64, 128), F32),
            pltpu.VMEM((zn, width // 64, 128), F32),
            pltpu.VMEM((2 * zn, width), F32),
            pltpu.VMEM((xn, 2 * zn, width), F32),
            pltpu.VMEM((groups, block, width), F32),
            pltpu.VMEM((yn, block, width), F32),
            pltpu.VMEM((half_y + 1, block, width), F32),
            pltpu.VMEM((half_y + 1, block, width), F32),
            pltpu.VMEM((half_y + 1, block, width), F32),
            pltpu.VMEM((half_y + 1, block, width), F32),
            pltpu.VMEM((xn, 2 * zn, width), F32),
            pltpu.VMEM((xn, 2 * zn, width), F32),
            pltpu.VMEM((zn, width // 64, 128), F32),
            pltpu.VMEM((zn, width // 64, 128), F32),
            dma((2, 2)),
            dma((2, zn)),
            dma((2, xn)),
            dma((2, half_y + 1)),
            dma((2, half_y + 1)),
            dma((2, yn)),
            dma((2, yn)),
            dma((2, half_y + 1)),
            dma((2, half_y + 1)),
            dma((2, xn)),
            dma((2, zn)),
        ],
        compiler_params=pltpu.CompilerParams(
            collective_id=0, has_side_effects=True, vmem_limit_bytes=56 * 1024 * 1024
        ),
    )(features, cotangent, w_self, w_neigh, bias.reshape(1, width), neighbours.T, lst, hub_local)


def solution(mesh):
    rows = P(("group", "dom"), None)
    return jax.shard_map(
        body,
        mesh=mesh,
        in_specs=(rows, rows, P(), P(), P(), rows, P(("group", "dom"), None, None), P(("group", "dom"))),
        out_specs=(rows, rows),
        check_vma=False,
    )
```

```python
import functools

import jax
import jax.numpy as jnp
from jax import lax
from jax.experimental import pallas as pl
from jax.experimental.pallas import tpu as pltpu
from jax.sharding import PartitionSpec as P

ZN = 12
F32 = jnp.float32
BF16 = jnp.bfloat16


def dot_t(left, right):
    return lax.dot_general(left, right, (((0,), (0,)), ((), ())), preferred_element_type=F32)


def dot_b(left, right):
    return lax.dot_general(left, right, (((1,), (1,)), ((), ())), preferred_element_type=F32)


def dot(left, right):
    return jnp.dot(left, right, preferred_element_type=F32)


def kernel(
    yn, xn, zn, feat, cot, ws, wn, bias, nbrt, lst, hubl, out, gout,
    tab, sel, zrows, xsend, arr, gsend, gback, zout, zin, hubtab,
    ha_s, ha, hb_s, hb, hubg, sib, ysr, yrr, ysl, yrl, xb_s, xb, za_s, za,
    sem_z, sem_rz, sem_x, sem_xg, sem_ha, sem_hb, sem_y, sem_sib, sem_sibg, sem_ry, sem_xb, sem_za,
):
    verts, width = feat.shape
    fanout = nbrt.shape[0]
    slots = arr.shape[2]
    lanes = 128
    tall = xn * slots
    quarter = width // lanes
    near = zn * tall
    hub_at = verts + near
    group = lax.axis_index("group")
    dom = lax.axis_index("dom")
    y, core = group // 2, lax.rem(group, 2)
    x, z = dom // zn, lax.rem(dom, zn)
    half_y, half_z = yn // 2, zn // 2
    cut = verts // 2

    def up_y(step):
        return lax.rem(y + step + 2 * yn, yn)

    def up_z(step):
        return lax.rem(z + step + 2 * zn, zn)

    def copy(src, dst, sems, at, **to):
        return pltpu.make_async_remote_copy(
            src_ref=src, dst_ref=dst, send_sem=sems.at[(0,) + at], recv_sem=sems.at[(1,) + at],
            device_id=to, device_id_type=pl.DeviceIdType.MESH,
        )

    def loop(lo, hi, body):
        lax.fori_loop(lo, hi, lambda i, c: (body(i), c)[1], 0)

    y_next = {1: {"group": up_y(1) * 2 + core}, -1: {"group": up_y(-1) * 2 + core}}
    z_next = {1: {"dom": x * zn + up_z(1)}, -1: {"dom": x * zn + up_z(-1)}}
    sibling = {"group": y * 2 + 1 - core}

    barrier = pltpu.get_barrier_semaphore()

    def greet(**to):
        pl.semaphore_signal(barrier, 1, device_id=to, device_id_type=pl.DeviceIdType.MESH)

    loop(1, zn, lambda i: greet(dom=x * zn + up_z(i)))
    for i in range(1, xn):
        greet(dom=lax.rem(x + i, xn) * zn + z)
    for partner in (y_next[1], y_next[-1], sibling):
        greet(**partner)

    row_id = lax.broadcasted_iota(jnp.int32, (16, verts), 0)
    vert_id = lax.broadcasted_iota(jnp.int32, (16, verts), 1)
    hub0, hub1 = hubl[0], hubl[1]
    wanted = jnp.where(row_id == 0, hub0, jnp.where(row_id == 1, hub1, -1))
    hub_rows = dot((vert_id == wanted).astype(BF16), feat[...])
    tile = 2 * quarter
    for zz in range(zn):
        for q in range(quarter):
            ha_s[zz, 2 * q:2 * q + 2, :] = hub_rows[0:2, q * lanes:(q + 1) * lanes]
        ha_s[zz, tile:tile + 8, :] = jnp.broadcast_to(lst[zz:zz + 1, :], (8, tall))
    ha[z] = ha_s[z]

    def tally(i):
        sub = lax.broadcasted_iota(jnp.int32, (tall, verts), 0)
        at = i * tall
        zz = i - verts // tall
        border = verts + zz * slots + (sub // slots) * (zn * slots) + lax.rem(sub, slots)
        is_border = jnp.logical_and(zz >= 0, zz < zn)
        rows = jnp.where(is_border, border, at + sub)
        total = jnp.zeros((tall, verts), F32)
        for e in range(fanout):
            total = jnp.where(nbrt[e:e + 1, :] == rows, total + 1.0, total)
        tab[pl.ds(pl.multiple_of(at, tall), tall), :] = total.astype(BF16)

    tiles = tab.shape[0] // tall
    spots = 2 * half_z + 1
    cuts = [tiles * k // spots for k in range(spots + 1)]

    def tally_part(k):
        loop(cuts[k], cuts[k + 1], tally)

    tally_part(0)
    pl.semaphore_wait(barrier, zn - 1 + xn - 1 + 3)

    def send_z(way, hop, part):
        owner = up_z(way * (1 - hop))
        rows = pl.ds(part * cut, cut)
        src = feat if hop == 1 else zrows.at[owner]
        return copy(src.at[rows], zrows.at[owner, rows], sem_z, (way + 1, hop, part), **z_next[way])

    def goes(way, hop, part):
        return hop < half_z or (hop == half_z and part == (0 if way > 0 else 1))

    def send_ha(i):
        to = up_z(i)
        return copy(ha_s.at[to], ha.at[z], sem_ha, (i,), dom=x * zn + to)

    loop(1, zn, lambda i: send_ha(i).start())
    for part, way in ((0, 1), (1, -1), (1, 1), (0, -1)):
        if goes(way, 1, part):
            send_z(way, 1, part).start()

    sub_id = lax.broadcasted_iota(jnp.int32, (verts, tall), 0).astype(F32)

    def pick(zz, rows):
        chosen = (sub_id == ha[zz, tile:tile + 1, :]).astype(BF16)
        sel[zz] = chosen
        xsend[zz] = dot_t(chosen, rows).astype(BF16).reshape(xn, slots, width)
        arr[zz, x] = xsend[zz, x]
        for i in range(1, xn):
            to = lax.rem(x + i, xn)
            copy(xsend.at[zz, to], arr.at[zz, x], sem_x, (0,), dom=to * zn + z).start()

    def hub_z():
        loop(1, zn, lambda i: send_ha(i).wait())
        for zz in range(zn):
            for q in range(quarter):
                hb_s[2 * zz:2 * zz + 2, q * lanes:(q + 1) * lanes] = ha[zz, 2 * q:2 * q + 2, :]
        hb[x] = hb_s[...]
        for i in range(1, xn):
            send_hb(i).start()

    def send_hb(i):
        return copy(hb_s, hb.at[x], sem_hb, (i,), dom=lax.rem(x + i, xn) * zn + z)

    block = hubtab.shape[1]

    def send_y(way, hop):
        owner = up_y(way * (1 - hop))
        part = hubtab.at[owner * 2 + core]
        if hop == half_y:
            part = part.at[pl.ds(0 if way > 0 else block // 2, block // 2)]
        return copy(part, part, sem_y, (way + 1, hop), **y_next[way])

    def send_sib(at, owner_y):
        part = hubtab.at[owner_y * 2 + core]
        return copy(part, part, sem_sib, (at,), **sibling)

    def hub_x():
        for i in range(1, xn):
            send_hb(i).wait()
        hubtab[group] = hb[...].reshape(block, width).astype(BF16)
        send_y(1, 1).start()
        send_y(-1, 1).start()
        send_sib(0, y).start()

    def hub_y(hop):
        send_y(1, hop).wait_recv()
        send_y(-1, hop).wait_recv()
        if hop < half_y:
            send_y(1, hop + 1).start()
            send_y(-1, hop + 1).start()
            send_sib(2 * hop - 1, up_y(-hop)).start()
            send_sib(2 * hop, up_y(hop)).start()
        else:
            send_sib(2 * hop - 1, up_y(hop)).start()

    hub_steps = [hub_z, hub_x] + [functools.partial(hub_y, hop) for hop in range(1, half_y + 1)]
    spot = 0
    for hop in range(1, half_z + 1):
        for turn, pair in enumerate((((1, 0), (-1, 1)), ((1, 1), (-1, 0)))):
            for way, part in pair:
                if goes(way, hop, part):
                    send_z(way, hop, part).wait_recv()
                    if goes(way, hop + 1, part):
                        send_z(way, hop + 1, part).start()
            if turn == 0:
                if hop == 1:
                    pick(z, feat[...])
                else:
                    pick(up_z(1 - hop), zrows[up_z(1 - hop)])
            elif hop > 1:
                pick(up_z(hop - 1), zrows[up_z(hop - 1)])
            if hub_steps:
                hub_steps.pop(0)()
            spot += 1
            tally_part(spot)
    pick(up_z(half_z), zrows[up_z(half_z)])
    while hub_steps:
        hub_steps.pop(0)()

    agg = dot_t(tab[0:verts, :], feat[...])
    pre = dot(feat[...], ws[...]) + bias[...]
    for i in range(yn):
        send_sib(i, y).wait()
    agg += dot_t(tab[hub_at:, :], hubtab[...].reshape(2 * yn * block, width))
    if xn > 1:
        most = (pl.ds(0, zn), pl.ds(0, xn - 1))
        copy(xsend.at[most], arr.at[most], sem_x, (0,), dom=lax.rem(x + 1, xn) * zn + z).wait()
    agg += dot_t(tab[verts:hub_at, :], arr[...].reshape(near, width))

    mean = (agg / fanout).astype(BF16)
    pre += dot(mean, wn[...])
    sigm = jax.nn.sigmoid(pre)
    out[...] = (pre * sigm).astype(BF16)
    grad_pre = (cot[...].astype(F32) * sigm * (1.0 + pre * (1.0 - sigm))).astype(BF16)
    grad_mean = (dot_b(grad_pre, wn[...]) / fanout).astype(BF16)

    def give(t):
        j = lax.rem(jnp.where(lax.rem(t, 2) == 1, half_z - (t + 1) // 2, t // 2 - half_z) + zn, zn)
        zz = up_z(j)
        rows = pl.ds(pl.multiple_of(verts + zz * tall, tall), tall)
        gsend[zz] = dot(tab[rows, :], grad_mean).astype(BF16).reshape(xn, slots, width)
        gback[zz, x] = gsend[zz, x]
        for i in range(1, xn):
            to = lax.rem(x + i, xn)
            copy(gsend.at[zz, to], gback.at[zz, x], sem_xg, (j,), dom=to * zn + z).start()

    loop(0, zn, give)
    hubg[...] = dot(tab[hub_at:, :], grad_mean).reshape(2 * yn, block, width)

    def send_sibg(i):
        owner = up_y(i)
        return copy(hubg.at[owner * 2 + 1 - core], sib.at[owner], sem_sibg, (i,), **sibling)

    order = [half_y]
    for i in range(half_y - 1, 0, -1):
        order += [i, yn - i]
    order += [0]
    for i in order:
        send_sibg(i).start()

    def given(j):
        some = pl.ds(0, xn - 1)
        zz = up_z(j)
        return copy(gsend.at[zz, some], gback.at[zz, some], sem_xg, (j % zn,), dom=lax.rem(x + 1, xn) * zn + z)

    def owed(j):
        if xn > 1:
            given(j).wait_recv()
        zz = up_z(j)
        return dot(sel[zz], gback[zz].reshape(tall, width))

    def send_g(way, hop, part):
        at, rows = (way + 1) // 2, pl.ds(part * cut, cut)
        return copy(zout.at[at, hop, rows], zin.at[at, hop, rows], sem_rz, (way + 1, hop, part), **z_next[way])

    def start_z():
        far = owed(half_z)
        for way, part in ((1, 0), (-1, 1)):
            rows = slice(part * cut, (part + 1) * cut)
            zout[(way + 1) // 2, half_z, rows] = far[rows].astype(BF16)
            send_g(way, half_z, part).start()

    def step_z(hop):
        terms = {1: owed(hop), -1: owed(-hop)}
        for way, part in ((1, 1), (-1, 0), (1, 0), (-1, 1)):
            rows = slice(part * cut, (part + 1) * cut)
            value = terms[way][rows]
            if goes(way, hop + 1, part):
                send_g(way, hop + 1, part).wait_recv()
                value = value + zin[(way + 1) // 2, hop + 1, rows].astype(F32)
            zout[(way + 1) // 2, hop, rows] = value.astype(BF16)
            send_g(way, hop, part).start()

    def mine(step):
        owner = up_y(step)
        return hubg[owner * 2 + core] + sib[owner]

    def send_h(way, k):
        src, dst = (ysr, yrr) if way > 0 else (ysl, yrl)
        src, dst = src.at[k], dst.at[k]
        if k == half_y:
            part = pl.ds(0 if way > 0 else block // 2, block // 2)
            src, dst = src.at[part], dst.at[part]
        return copy(src, dst, sem_ry, (way + 1, k), **y_next[way])

    lower, upper = slice(0, block // 2), slice(block // 2, block)

    def start_y():
        send_sibg(half_y).wait_recv()
        far = mine(half_y)
        ysr[half_y, lower] = far[lower]
        ysl[half_y, upper] = far[upper]
        send_h(1, half_y).start()
        send_h(-1, half_y).start()

    def step_y(k):
        for i in sorted({k, (yn - k) % yn}):
            send_sibg(i).wait_recv()
        send_h(1, k + 1).wait_recv()
        send_h(-1, k + 1).wait_recv()
        if k == half_y - 1:
            if k > 0:
                on_r, on_l = mine(k), mine(-k)
                ysr[k, lower] = on_r[lower] + yrr[k + 1, lower]
                ysr[k, upper] = on_r[upper]
                ysl[k, lower] = on_l[lower]
                ysl[k, upper] = on_l[upper] + yrl[k + 1, upper]
            else:
                total = mine(0)
                ysr[0, lower] = total[lower] + yrr[1, lower]
                ysr[0, upper] = total[upper] + yrl[1, upper]
        elif k > 0:
            ysr[k] = mine(k) + yrr[k + 1]
            ysl[k] = mine(-k) + yrl[k + 1]
        else:
            ysr[0] = mine(0) + yrr[1] + yrl[1]
        if k > 0:
            send_h(1, k).start()
            send_h(-1, k).start()

    def send_xb(i):
        to = lax.rem(x + i, xn)
        return copy(xb_s.at[to], xb.at[i], sem_xb, (i,), dom=to * zn + z)

    def send_za(i):
        to = up_z(i)
        return copy(za_s.at[to], za.at[i], sem_za, (i,), dom=x * zn + to)

    def start_x():
        xb_s[...] = ysr[0].reshape(xn, 2 * zn, width)
        for i in range(1, xn):
            send_xb(i).start()

    def end_x():
        total = xb_s[x]
        for i in range(1, xn):
            send_xb(i).wait_recv()
            total = total + xb[i]
        for zz in range(zn):
            for q in range(quarter):
                za_s[zz, 2 * q:2 * q + 2, :] = total[2 * zz:2 * zz + 2, q * lanes:(q + 1) * lanes]
        loop(1, zn, lambda i: send_za(i).start())

    def self_part():
        gout[...] = dot(tab[0:verts, :], grad_mean) + dot_b(grad_pre, ws[...])

    jobs = [self_part, start_y] + [functools.partial(step_y, k) for k in range(half_y - 1, -1, -1)] + [start_x, end_x]
    per_step = -(-len(jobs) // half_z)
    start_z()
    for hop in range(half_z - 1, -1, -1):
        for job in jobs[:per_step]:
            job()
        jobs = jobs[per_step:]
        if hop > 0:
            step_z(hop)
    for job in jobs:
        job()
    gout[...] += owed(0)
    for way, part in ((1, 1), (-1, 0), (1, 0), (-1, 1)):
        if goes(way, 1, part):
            rows = slice(part * cut, (part + 1) * cut)
            send_g(way, 1, part).wait_recv()
            gout[rows, :] += zin[(way + 1) // 2, 1, rows].astype(F32)
    loop(1, zn, lambda i: send_za(i).wait_recv())
    hub_sum = za_s[z]
    for i in range(1, zn):
        hub_sum = hub_sum + za[i]
    rows_of = lax.broadcasted_iota(jnp.int32, (verts, lanes), 0)
    for q in range(quarter):
        cols = slice(q * lanes, (q + 1) * lanes)
        gout[:, cols] += jnp.where(rows_of == hub0, hub_sum[2 * q:2 * q + 1], 0.0) + jnp.where(
            rows_of == hub1, hub_sum[2 * q + 1:2 * q + 2], 0.0
        )

    for hop in range(1, half_z + 1):
        for way, part in ((1, 0), (1, 1), (-1, 0), (-1, 1)):
            if goes(way, hop, part):
                send_z(way, hop, part).wait_send()
                send_g(way, hop, part).wait_send()
    for hop in range(1, half_y + 1):
        for way in (1, -1):
            send_y(way, hop).wait_send()
            send_h(way, hop).wait_send()
    for i in range(yn):
        send_sibg(i).wait_send()
    if xn > 1:
        for j in range(zn):
            given(j).wait_send()
    for i in range(1, xn):
        send_xb(i).wait_send()
    loop(1, zn, lambda i: send_za(i).wait_send())


def body(features, cotangent, w_self, w_neigh, bias, neighbours, send_rows, hub_local):
    verts, width = features.shape
    peers, slots = send_rows.shape[1:]
    xn, zn = peers // ZN, ZN
    groups = lax.axis_size("group")
    yn = groups // 2
    half_y, half_z = yn // 2, zn // 2
    near = peers * slots
    tall = xn * slots
    block = 2 * peers
    tile = width // 64
    lst = send_rows.reshape(xn, zn, slots).transpose(1, 0, 2).reshape(zn, tall).astype(F32)
    vmem = pl.BlockSpec(memory_space=pltpu.VMEM)
    dma = pltpu.SemaphoreType.DMA
    edge = (zn, xn, slots, width)
    ring = (half_y + 1, block, width)
    return pl.pallas_call(
        functools.partial(kernel, yn, xn, zn),
        out_shape=(
            jax.ShapeDtypeStruct((verts, width), BF16),
            jax.ShapeDtypeStruct((verts, width), F32),
        ),
        in_specs=[vmem] * 7 + [pl.BlockSpec(memory_space=pltpu.SMEM)],
        out_specs=(vmem, vmem),
        scratch_shapes=[
            pltpu.VMEM((verts + near + groups * block, verts), BF16),
            pltpu.VMEM((zn, verts, tall), BF16),
            pltpu.VMEM((zn, verts, width), BF16),
            pltpu.VMEM(edge, BF16),
            pltpu.VMEM(edge, BF16),
            pltpu.VMEM(edge, BF16),
            pltpu.VMEM(edge, BF16),
            pltpu.VMEM((2, half_z + 1, verts, width), BF16),
            pltpu.VMEM((2, half_z + 1, verts, width), BF16),
            pltpu.VMEM((groups, block, width), BF16),
            pltpu.VMEM((zn, tile + 8, 128), F32),
            pltpu.VMEM((zn, tile + 8, 128), F32),
            pltpu.VMEM((2 * zn, width), F32),
            pltpu.VMEM((xn, 2 * zn, width), F32),
            pltpu.VMEM((groups, block, width), F32),
            pltpu.VMEM((yn, block, width), F32),
            pltpu.VMEM(ring, F32),
            pltpu.VMEM(ring, F32),
            pltpu.VMEM(ring, F32),
            pltpu.VMEM(ring, F32),
            pltpu.VMEM((xn, 2 * zn, width), F32),
            pltpu.VMEM((xn, 2 * zn, width), F32),
            pltpu.VMEM((zn, tile, 128), F32),
            pltpu.VMEM((zn, tile, 128), F32),
            dma((2, 3, half_z + 1, 2)),
            dma((2, 3, half_z + 1, 2)),
            dma((2, 1)),
            dma((2, zn)),
            dma((2, zn)),
            dma((2, xn)),
            dma((2, 3, half_y + 1)),
            dma((2, yn)),
            dma((2, yn)),
            dma((2, 3, half_y + 1)),
            dma((2, xn)),
            dma((2, zn)),
        ],
        compiler_params=pltpu.CompilerParams(
            collective_id=0, has_side_effects=True, vmem_limit_bytes=60 * 1024 * 1024
        ),
    )(features, cotangent, w_self, w_neigh, bias.reshape(1, width), neighbours.T, lst, hub_local)


def solution(mesh):
    rows = P(("group", "dom"), None)
    return jax.shard_map(
        body,
        mesh=mesh,
        in_specs=(rows, rows, P(), P(), P(), rows, P(("group", "dom"), None, None), P(("group", "dom"))),
        out_specs=(rows, rows),
        check_vma=False,
    )
```

```python
import functools

import jax
import jax.numpy as jnp
from jax import lax
from jax.experimental import pallas as pl
from jax.experimental.pallas import tpu as pltpu
from jax.sharding import PartitionSpec as P

ZN = 12
PARTS = 2
F32 = jnp.float32
BF16 = jnp.bfloat16


def dot_t(left, right):
    return lax.dot_general(left, right, (((0,), (0,)), ((), ())), preferred_element_type=F32)


def dot_b(left, right):
    return lax.dot_general(left, right, (((1,), (1,)), ((), ())), preferred_element_type=F32)


def dot(left, right):
    return jnp.dot(left, right, preferred_element_type=F32)


def kernel(
    yn, xn, zn, feat, cot, ws, wn, bias, nbrt, lst, hubl, out, gout,
    tab, sel, sel_b, rel, lists, zrows, xsend, bsend, arr, gsend, gback, gback_b, zout, zin, hubtab,
    ha_s, ha, hb_s, hb, hubg, sib_s, sib, yg_s, yg, xb_s, xb, za_s, za,
    sem_z, sem_rz, sem_l, sem_x, sem_b, sem_xg, sem_gb, sem_ha, sem_hb, sem_y, sem_sib, sem_sibg, sem_yg, sem_xb, sem_za,
):
    verts, width = feat.shape
    fanout = nbrt.shape[0]
    slots = arr.shape[2]
    lanes = 128
    tall = xn * slots
    quarter = width // lanes
    near = zn * tall
    hub_at = verts + near
    group = lax.axis_index("group")
    dom = lax.axis_index("dom")
    y, core = group // 2, lax.rem(group, 2)
    x, z = dom // zn, lax.rem(dom, zn)
    half_z = zn // 2
    hops = half_z - 2
    parts = sem_z.shape[3]
    cut = verts // parts

    def up_y(step):
        return lax.rem(y + step + 2 * yn, yn)

    def up_z(step):
        return lax.rem(z + step + 2 * zn, zn)

    def copy(src, dst, sems, at, **to):
        return pltpu.make_async_remote_copy(
            src_ref=src, dst_ref=dst, send_sem=sems.at[(0,) + at], recv_sem=sems.at[(1,) + at],
            device_id=to, device_id_type=pl.DeviceIdType.MESH,
        )

    def loop(lo, hi, body):
        lax.fori_loop(lo, hi, lambda i, c: (body(i), c)[1], 0)

    z_next = {1: {"dom": x * zn + up_z(1)}, -1: {"dom": x * zn + up_z(-1)}}
    sibling = {"group": y * 2 + 1 - core}

    barrier = pltpu.get_barrier_semaphore()

    def greet(**to):
        pl.semaphore_signal(barrier, 1, device_id=to, device_id_type=pl.DeviceIdType.MESH)

    loop(1, zn, lambda i: greet(dom=x * zn + up_z(i)))
    for i in range(1, xn):
        greet(dom=lax.rem(x + i, xn) * zn + z)
        for step in (-2, -1, 1, 2):
            greet(dom=lax.rem(x + i, xn) * zn + up_z(step))
    for i in range(1, yn):
        greet(group=up_y(i) * 2 + core)
    greet(**sibling)

    row_id = lax.broadcasted_iota(jnp.int32, (16, verts), 0)
    vert_id = lax.broadcasted_iota(jnp.int32, (16, verts), 1)
    hub0, hub1 = hubl[0], hubl[1]
    wanted = jnp.where(row_id == 0, hub0, jnp.where(row_id == 1, hub1, -1))
    hub_rows = dot((vert_id == wanted).astype(BF16), feat[...])
    for q in range(quarter):
        ha_s[2 * q:2 * q + 2, :] = hub_rows[0:2, q * lanes:(q + 1) * lanes]
    ha[z] = ha_s[...]
    rel[...] = jnp.full_like(rel, -1.0)
    for d in range(zn):
        rel[d:d + 1, :] = lst[pl.ds(up_z(d), 1), :]
    lists[z] = rel[...].astype(BF16)

    def tally(i):
        sub = lax.broadcasted_iota(jnp.int32, (tall, verts), 0)
        at = i * tall
        zz = i - verts // tall
        border = verts + zz * slots + (sub // slots) * (zn * slots) + lax.rem(sub, slots)
        is_border = jnp.logical_and(zz >= 0, zz < zn)
        rows = jnp.where(is_border, border, at + sub)
        total = jnp.zeros((tall, verts), F32)
        for e in range(fanout):
            total = jnp.where(nbrt[e:e + 1, :] == rows, total + 1.0, total)
        tab[pl.ds(pl.multiple_of(at, tall), tall), :] = total.astype(BF16)

    tiles = tab.shape[0] // tall
    spots = 2 * hops + 1
    cuts = [tiles * k // spots for k in range(spots + 1)]

    def tally_part(k):
        loop(cuts[k], cuts[k + 1], tally)

    tally_part(0)
    pl.semaphore_wait(barrier, zn - 1 + 5 * (xn - 1) + yn)

    def send_z(way, hop, part):
        owner = up_z(way * (1 - hop))
        rows = pl.ds(part * cut, cut)
        src = feat if hop == 1 else zrows.at[owner]
        return copy(src.at[rows], zrows.at[owner, rows], sem_z, (way + 1, hop, part), **z_next[way])

    def turns(first):
        for t in range(parts):
            part = (t + first) % parts
            yield 1, part
            yield -1, parts - 1 - part

    def send_ha(i):
        to = up_z(i)
        return copy(ha_s, ha.at[z], sem_ha, (i,), dom=x * zn + to)

    def send_l(way, hop):
        owner = lists.at[up_z(way * (1 - hop))]
        return copy(owner, owner, sem_l, (way + 1, hop), **z_next[way])

    loop(1, zn, lambda i: send_ha(i).start())
    send_l(1, 1).start()
    send_l(-1, 1).start()
    for way, part in turns(0):
        send_z(way, 1, part).start()

    sub_id = lax.broadcasted_iota(jnp.int32, (verts, tall), 0).astype(F32)

    def chosen_rows(owner, d, rows, sel_at, to_at):
        chosen = (sub_id == lists[owner, d % zn:d % zn + 1, :].astype(F32)).astype(BF16)
        sel_at[...] = chosen
        to_at[...] = dot_t(chosen, rows).astype(BF16).reshape(xn, slots, width)

    def pick(j):
        zz = up_z(j)
        chosen_rows(zz, -j, feat[...] if j == 0 else zrows[zz], sel.at[zz], xsend.at[zz])
        arr[zz, x] = xsend[zz, x]
        for i in range(1, xn):
            to = lax.rem(x + i, xn)
            copy(xsend.at[zz, to], arr.at[zz, x], sem_x, (0,), dom=to * zn + z).start()

    def far_of(way):
        return range(xn // 2) if way > 0 else range(xn // 2, xn)

    def b_slot(way, step):
        return (way + 1) // 2 if step == 1 else 2

    def pick_beyond(way, step):
        side, slot = (way + 1) // 2, b_slot(way, step)
        owner = up_z(-way * hops)
        rows = bsend.at[side, step - 1]
        chosen_rows(owner, way * (hops + step), zrows[owner], sel_b.at[side, step - 1], rows)
        for to in range(xn) if step == 1 else far_of(way):
            pltpu.make_async_remote_copy(
                src_ref=rows.at[to], dst_ref=arr.at[owner, x], send_sem=sem_b.at[0, slot, to], recv_sem=sem_b.at[1, slot, x],
                device_id={"dom": to * zn + up_z(way * step)}, device_id_type=pl.DeviceIdType.MESH,
            ).start()

    def hub_z():
        loop(1, zn, lambda i: send_ha(i).wait())
        for zz in range(zn):
            for q in range(quarter):
                hb_s[2 * zz:2 * zz + 2, q * lanes:(q + 1) * lanes] = ha[zz, 2 * q:2 * q + 2, :]
        hb[x] = hb_s[...]
        for i in range(1, xn):
            send_hb(i).start()

    def send_hb(i):
        return copy(hb_s, hb.at[x], sem_hb, (i,), dom=lax.rem(x + i, xn) * zn + z)

    block = hubtab.shape[1]

    def send_y(i):
        mine = hubtab.at[group]
        return copy(mine, mine, sem_y, (i,), group=up_y(i) * 2 + core)

    def send_sib(i):
        part = hubtab.at[up_y(-i) * 2 + core]
        return copy(part, part, sem_sib, (i,), **sibling)

    y_order = sorted(range(1, yn), key=lambda i: min(i, yn - i))

    def hub_x():
        for i in range(1, xn):
            send_hb(i).wait()
        hubtab[group] = hb[...].reshape(block, width).astype(BF16)
        for i in y_order:
            send_y(i).start()
        send_sib(0).start()

    def hub_y(some):
        for i in some:
            send_y(i).wait_recv()
            send_sib(i).start()

    near_y = (len(y_order) + 1) // 2
    last = 2 * hops - 1
    hub_steps = [
        (min(1, last), hub_z), (min(3, last), hub_x), (last, lambda: hub_y(y_order[:near_y])),
    ]
    spot = 0
    for hop in range(1, hops + 1):
        for t, (way, part) in enumerate(turns(0)):
            if t < 2:
                send_l(way, hop).wait_recv()
                if hop < hops:
                    send_l(way, hop + 1).start()
            send_z(way, hop, part).wait_recv()
            if hop < hops:
                send_z(way, hop + 1, part).start()
            if t == parts - 1:
                pick(1 - hop)
            elif t == 2 * parts - 1 and hop > 1:
                pick(hop - 1)
            if t % parts == parts - 1 and spot < last:
                for at, step in hub_steps:
                    if at == spot:
                        step()
                spot += 1
                tally_part(spot)
    for step in (2, 1):
        for way in (1, -1):
            pick_beyond(way, step)
    pick(-hops)
    pick(hops)
    for at, step in hub_steps:
        if at == spot:
            step()
    tally_part(spot + 1)
    hub_y(y_order[near_y:])

    agg = dot_t(tab[0:verts, :], feat[...])
    pre = dot(feat[...], ws[...]) + bias[...]
    for i in range(yn):
        send_sib(i).wait()
    agg += dot_t(tab[hub_at:, :], hubtab[...].reshape(2 * yn * block, width))
    if xn > 1:
        most = (pl.ds(0, 2 * hops + 1), pl.ds(0, xn - 1))
        copy(xsend.at[most], arr.at[most], sem_x, (0,), dom=lax.rem(x + 1, xn) * zn + z).wait()
    for slot in range(3):
        for i in range(xn):
            copy(bsend.at[0, 0, 0], arr.at[0, i], sem_b, (slot, i), **sibling).wait()
    agg += dot_t(tab[verts:hub_at, :], arr[...].reshape(near, width))

    mean = (agg / fanout).astype(BF16)
    pre += dot(mean, wn[...])
    sigm = jax.nn.sigmoid(pre)
    out[...] = (pre * sigm).astype(BF16)
    grad_pre = (cot[...].astype(F32) * sigm * (1.0 + pre * (1.0 - sigm))).astype(BF16)
    grad_mean = (dot_b(grad_pre, wn[...]) / fanout).astype(BF16)

    def slot_grads(zz):
        rows = pl.ds(pl.multiple_of(verts + zz * tall, tall), tall)
        gsend[zz] = dot(tab[rows, :], grad_mean).astype(BF16).reshape(xn, slots, width)

    def give_beyond(side, step, slot, to):
        way = 2 * side - 1
        return pltpu.make_async_remote_copy(
            src_ref=gsend.at[up_z(-way * (hops + step)), to], dst_ref=gback_b.at[side, step - 1, x],
            send_sem=sem_gb.at[0, slot, to], recv_sem=sem_gb.at[1, slot, x],
            device_id={"dom": to * zn + up_z(-way * step)}, device_id_type=pl.DeviceIdType.MESH,
        )

    my_side = 1 - x // (xn // 2)
    beyond = [(my_side, 2, 2), (1, 1, 1), (0, 1, 0)]
    for side, step, slot in beyond:
        slot_grads(up_z((1 - 2 * side) * (hops + step)))
        for to in range(xn):
            give_beyond(side, step, slot, to).start()
    gback_b[1, 1, xn // 2:] = jnp.zeros((xn // 2, slots, width), BF16)
    gback_b[0, 1, :xn // 2] = jnp.zeros((xn // 2, slots, width), BF16)

    def send_sibg(owner):
        return copy(sib_s.at[owner], sib.at[owner], sem_sibg, (owner,), **sibling)

    def hub_terms(owner):
        rows = pl.ds(pl.multiple_of(hub_at + owner * 2 * block, 32), 2 * block)
        hubg[pl.ds(2 * owner, 2)] = dot(tab[rows, :], grad_mean).reshape(2, block, width)
        sib_s[owner] = hubg[2 * owner + 1 - core].astype(BF16)
        send_sibg(owner).start()

    loop(0, yn, hub_terms)

    def give(t):
        j = lax.rem(jnp.where(lax.rem(t, 2) == 1, half_z - (t + 1) // 2, t // 2 - half_z) + zn, zn)
        zz = up_z(j)
        slot_grads(zz)
        gback[zz, x] = gsend[zz, x]
        for i in range(1, xn):
            to = lax.rem(x + i, xn)
            copy(gsend.at[zz, to], gback.at[zz, x], sem_xg, (j,), dom=to * zn + z).start()

    loop(3, zn, give)

    def given(j):
        some = pl.ds(0, xn - 1)
        zz = up_z(j)
        return copy(gsend.at[zz, some], gback.at[zz, some], sem_xg, (j % zn,), dom=lax.rem(x + 1, xn) * zn + z)

    def owed(j):
        if xn > 1:
            given(j).wait_recv()
        zz = up_z(j)
        value = dot(sel[zz], gback[zz].reshape(tall, width))
        if abs(j) == hops:
            way = 1 if j < 0 else -1
            side = (way + 1) // 2
            for step in (1, 2):
                slot = b_slot(way, step)
                for i in range(xn) if step == 1 else far_of(way):
                    copy(gsend.at[0, 0], gback_b.at[side, step - 1, i], sem_gb, (slot, i), **sibling).wait_recv()
                value += dot(sel_b[side, step - 1], gback_b[side, step - 1].reshape(tall, width))
        return value

    def send_g(way, hop, part):
        at, rows = (way + 1) // 2, pl.ds(part * cut, cut)
        return copy(zout.at[at, hop, rows], zin.at[at, hop, rows], sem_rz, (way + 1, hop, part), **z_next[way])

    def step_z(hop):
        terms = {1: owed(hop), -1: owed(-hop)}
        for way, part in turns(0):
            rows = slice(part * cut, (part + 1) * cut)
            value = terms[way][rows]
            if hop < hops:
                send_g(way, hop + 1, part).wait_recv()
                value = value + zin[(way + 1) // 2, hop + 1, rows].astype(F32)
            zout[(way + 1) // 2, hop, rows] = value.astype(BF16)
            send_g(way, hop, part).start()

    def mine(owner):
        return hubg[owner * 2 + core] + sib[owner].astype(F32)

    def send_yg(i):
        return copy(yg_s.at[i], yg.at[i], sem_yg, (i,), group=up_y(i) * 2 + core)

    def start_y():
        loop(0, yn, lambda i: send_sibg(i).wait_recv())

        def give_y(i):
            yg_s[i] = mine(up_y(i)).astype(BF16)
            send_yg(i).start()

        loop(1, yn, give_y)

    def send_xb(i):
        to = lax.rem(x + i, xn)
        return copy(xb_s.at[to], xb.at[i], sem_xb, (i,), dom=to * zn + z)

    def send_za(i):
        to = up_z(i)
        return copy(za_s.at[to], za.at[i], sem_za, (i,), dom=x * zn + to)

    def start_x():
        total = mine(y)
        for i in range(1, yn):
            send_yg(i).wait_recv()
            total = total + yg[i].astype(F32)
        xb_s[...] = total.reshape(xn, 2 * zn, width)
        for i in range(1, xn):
            send_xb(i).start()

    def end_x():
        total = xb_s[x]
        for i in range(1, xn):
            send_xb(i).wait_recv()
            total = total + xb[i]
        for zz in range(zn):
            for q in range(quarter):
                za_s[zz, 2 * q:2 * q + 2, :] = total[2 * zz:2 * zz + 2, q * lanes:(q + 1) * lanes]
        loop(1, zn, lambda i: send_za(i).start())

    def self_part():
        gout[...] = dot(tab[0:verts, :], grad_mean) + dot_b(grad_pre, ws[...])

    jobs = [(hops, self_part), (min(2, hops), start_x), (1, end_x)]
    start_y()
    for hop in range(hops, 0, -1):
        step_z(hop)
        for at, job in jobs:
            if at == hop:
                job()
    gout[...] += owed(0)
    for way, part in turns(0):
        rows = slice(part * cut, (part + 1) * cut)
        send_g(way, 1, part).wait_recv()
        gout[rows, :] += zin[(way + 1) // 2, 1, rows].astype(F32)
    loop(1, zn, lambda i: send_za(i).wait_recv())
    hub_sum = za_s[z]
    for i in range(1, zn):
        hub_sum = hub_sum + za[i]
    rows_of = lax.broadcasted_iota(jnp.int32, (verts, lanes), 0)
    for q in range(quarter):
        cols = slice(q * lanes, (q + 1) * lanes)
        gout[:, cols] += jnp.where(rows_of == hub0, hub_sum[2 * q:2 * q + 1], 0.0) + jnp.where(
            rows_of == hub1, hub_sum[2 * q + 1:2 * q + 2], 0.0
        )

    for hop in range(1, hops + 1):
        for way, part in turns(0):
            send_z(way, hop, part).wait_send()
            send_g(way, hop, part).wait_send()
        send_l(1, hop).wait_send()
        send_l(-1, hop).wait_send()
    for i in range(1, yn):
        send_y(i).wait_send()
        send_yg(i).wait_send()
    for i in range(yn):
        send_sibg(i).wait_send()
    if xn > 1:
        for j in range(zn):
            if min(j, zn - j) <= hops:
                given(j).wait_send()
    for side, step, slot in beyond:
        for to in range(xn):
            give_beyond(side, step, slot, to).wait_send()
    for i in range(1, xn):
        send_xb(i).wait_send()
    loop(1, zn, lambda i: send_za(i).wait_send())


def body(features, cotangent, w_self, w_neigh, bias, neighbours, send_rows, hub_local):
    verts, width = features.shape
    peers, slots = send_rows.shape[1:]
    xn, zn = peers // ZN, ZN
    groups = lax.axis_size("group")
    yn = groups // 2
    half_z, parts = zn // 2, PARTS
    near = peers * slots
    tall = xn * slots
    block = 2 * peers
    tile = width // 64
    lst = send_rows.reshape(xn, zn, slots).transpose(1, 0, 2).reshape(zn, tall).astype(F32)
    vmem = pl.BlockSpec(memory_space=pltpu.VMEM)
    dma = pltpu.SemaphoreType.DMA
    edge = (zn, xn, slots, width)
    hub = (yn, block, width)
    return pl.pallas_call(
        functools.partial(kernel, yn, xn, zn),
        out_shape=(
            jax.ShapeDtypeStruct((verts, width), BF16),
            jax.ShapeDtypeStruct((verts, width), F32),
        ),
        in_specs=[vmem] * 7 + [pl.BlockSpec(memory_space=pltpu.SMEM)],
        out_specs=(vmem, vmem),
        scratch_shapes=[
            pltpu.VMEM((verts + near + groups * block, verts), BF16),
            pltpu.VMEM((zn, verts, tall), BF16),
            pltpu.VMEM((2, 2, verts, tall), BF16),
            pltpu.VMEM((16, tall), F32),
            pltpu.VMEM((zn, 16, tall), BF16),
            pltpu.VMEM((zn, verts, width), BF16),
            pltpu.VMEM(edge, BF16),
            pltpu.VMEM((2, 2) + edge[1:], BF16),
            pltpu.VMEM(edge, BF16),
            pltpu.VMEM(edge, BF16),
            pltpu.VMEM(edge, BF16),
            pltpu.VMEM((2, 2) + edge[1:], BF16),
            pltpu.VMEM((2, half_z - 1, verts, width), BF16),
            pltpu.VMEM((2, half_z - 1, verts, width), BF16),
            pltpu.VMEM((groups, block, width), BF16),
            pltpu.VMEM((tile, 128), F32),
            pltpu.VMEM((zn, tile, 128), F32),
            pltpu.VMEM((2 * zn, width), F32),
            pltpu.VMEM((xn, 2 * zn, width), F32),
            pltpu.VMEM((groups, block, width), F32),
            pltpu.VMEM(hub, BF16),
            pltpu.VMEM(hub, BF16),
            pltpu.VMEM(hub, BF16),
            pltpu.VMEM(hub, BF16),
            pltpu.VMEM((xn, 2 * zn, width), F32),
            pltpu.VMEM((xn, 2 * zn, width), F32),
            pltpu.VMEM((zn, tile, 128), F32),
            pltpu.VMEM((zn, tile, 128), F32),
            dma((2, 3, half_z, parts)),
            dma((2, 3, half_z, parts)),
            dma((2, 3, half_z)),
            dma((2, 1)),
            dma((2, 3, xn)),
            dma((2, zn)),
            dma((2, 3, xn)),
            dma((2, zn)),
            dma((2, xn)),
            dma((2, yn)),
            dma((2, yn)),
            dma((2, yn)),
            dma((2, yn)),
            dma((2, xn)),
            dma((2, zn)),
        ],
        compiler_params=pltpu.CompilerParams(
            collective_id=0, has_side_effects=True, vmem_limit_bytes=60 * 1024 * 1024
        ),
    )(features, cotangent, w_self, w_neigh, bias.reshape(1, width), neighbours.T, lst, hub_local)


def solution(mesh):
    rows = P(("group", "dom"), None)
    return jax.shard_map(
        body,
        mesh=mesh,
        in_specs=(rows, rows, P(), P(), P(), rows, P(("group", "dom"), None, None), P(("group", "dom"))),
        out_specs=(rows, rows),
        check_vma=False,
    )
```

```python
import functools

import jax
import jax.numpy as jnp
from jax import lax
from jax.experimental import pallas as pl
from jax.experimental.pallas import tpu as pltpu
from jax.sharding import PartitionSpec as P

ZN = 12
PARTS = 2
F32 = jnp.float32
BF16 = jnp.bfloat16


def dot_t(left, right):
    return lax.dot_general(left, right, (((0,), (0,)), ((), ())), preferred_element_type=F32)


def dot_b(left, right):
    return lax.dot_general(left, right, (((1,), (1,)), ((), ())), preferred_element_type=F32)


def dot(left, right):
    return jnp.dot(left, right, preferred_element_type=F32)


def kernel(
    yn, xn, zn, feat_in, cot_in, ws_in, wn_in, bias_in, nbrt_in, sr_in, hubl, out, gout,
    feat, cot, ws, wn, bias, nbrt, sr, lst, outv, gm,
    tab, sel, sel_b, rel, lists, zrows, xsend, bsend, arr, gsend, gback, gback_b, zout, zin, hubtab,
    ha_s, ha, hb_s, hb, hubg, sib_s, sib, yg_s, yg, xb_s, xb, za_s, za,
    sem_z, sem_rz, sem_l, sem_x, sem_b, sem_xg, sem_gb, sem_ha, sem_hb, sem_y, sem_sib, sem_sibg, sem_yg, sem_xb, sem_za, sem_in,
):
    verts, width = feat.shape
    fanout = nbrt.shape[0]
    slots = arr.shape[3]
    lanes = 128
    tall = xn * slots
    quarter = width // lanes
    near = zn * tall
    hub_at = verts + near
    group = lax.axis_index("group")
    dom = lax.axis_index("dom")
    y, core = group // 2, lax.rem(group, 2)
    x, z = dom // zn, lax.rem(dom, zn)
    half_z = zn // 2
    hops = half_z - 2
    parts = sem_z.shape[3]
    cut = width // parts

    def up_y(step):
        return lax.rem(y + step + 2 * yn, yn)

    def up_z(step):
        return lax.rem(z + step + 2 * zn, zn)

    def copy(src, dst, sems, at, **to):
        return pltpu.make_async_remote_copy(
            src_ref=src, dst_ref=dst, send_sem=sems.at[(0,) + at], recv_sem=sems.at[(1,) + at],
            device_id=to, device_id_type=pl.DeviceIdType.MESH,
        )

    def loop(lo, hi, body):
        lax.fori_loop(lo, hi, lambda i, c: (body(i), c)[1], 0)

    z_next = {1: {"dom": x * zn + up_z(1)}, -1: {"dom": x * zn + up_z(-1)}}
    sibling = {"group": y * 2 + 1 - core}

    barrier = pltpu.get_barrier_semaphore()

    def greet(**to):
        pl.semaphore_signal(barrier, 1, device_id=to, device_id_type=pl.DeviceIdType.MESH)

    loop(1, zn, lambda i: greet(dom=x * zn + up_z(i)))
    for i in range(1, xn):
        greet(dom=lax.rem(x + i, xn) * zn + z)
        for step in (-2, -1, 1, 2):
            greet(dom=lax.rem(x + i, xn) * zn + up_z(step))
    for step in (-2, -1, 1, 2):
        greet(group=up_y(step) * 2 + core)
    greet(**sibling)

    sources = (feat_in, sr_in, nbrt_in, cot_in, ws_in, wn_in, bias_in)
    loads = [
        pltpu.make_async_copy(src, dst, sem_in.at[i])
        for i, (src, dst) in enumerate(zip(sources, (feat, sr, nbrt, cot, ws, wn, bias)))
    ]
    for part in range(parts):
        cols = feat_in.at[:, pl.ds(part * cut, cut)]
        loads.append(pltpu.make_async_copy(cols, zrows.at[z, part], sem_in.at[7 + part]))
    for i in (0, 1, 7, 2, 3, 4, 5, 6):
        loads[i].start()
    for load in loads[8:]:
        load.start()
    loads[0].wait()

    row_id = lax.broadcasted_iota(jnp.int32, (16, verts), 0)
    vert_id = lax.broadcasted_iota(jnp.int32, (16, verts), 1)
    hub0, hub1 = hubl[0], hubl[1]
    wanted = jnp.where(row_id == 0, hub0, jnp.where(row_id == 1, hub1, -1))
    hub_rows = dot((vert_id == wanted).astype(BF16), feat[...])
    for q in range(quarter):
        ha_s[2 * q:2 * q + 2, :] = hub_rows[0:2, q * lanes:(q + 1) * lanes]
    ha[z] = ha_s[...]
    loads[1].wait()
    by_peer = sr[...].astype(F32).T
    for xx in range(xn):
        lst[:, xx * slots:(xx + 1) * slots] = by_peer[xx * zn:(xx + 1) * zn, :]
    rel[...] = jnp.full_like(rel, -1.0)
    for d in range(zn):
        rel[d:d + 1, :] = lst[pl.ds(up_z(d), 1), :]
    lists[z] = rel[...].astype(BF16)

    def tally(i):
        sub = lax.broadcasted_iota(jnp.int32, (tall, verts), 0)
        at = i * tall
        zz = i - verts // tall
        border = verts + zz * slots + (sub // slots) * (zn * slots) + lax.rem(sub, slots)
        is_border = jnp.logical_and(zz >= 0, zz < zn)
        rows = jnp.where(is_border, border, at + sub)
        total = jnp.zeros((tall, verts), F32)
        for e in range(fanout):
            total = jnp.where(nbrt[e:e + 1, :] == rows, total + 1.0, total)
        tab[pl.ds(pl.multiple_of(at, tall), tall), :] = total.astype(BF16)

    tiles = tab.shape[0] // tall
    spots = 2 * hops + 1
    cuts = [tiles * k // spots for k in range(spots + 1)]

    def tally_part(k):
        loop(cuts[k], cuts[k + 1], tally)

    loads[2].wait()
    tally_part(0)
    for load in loads[7:]:
        load.wait()
    pl.semaphore_wait(barrier, zn - 1 + 5 * (xn - 1) + 5)

    def send_z(way, hop, part):
        piece = zrows.at[up_z(way * (1 - hop)), part]
        return copy(piece, piece, sem_z, (way + 1, hop, part), **z_next[way])

    turns = [(way, part) for part in range(parts) for way in (1, -1)]

    def send_ha(i):
        to = up_z(i)
        return copy(ha_s, ha.at[z], sem_ha, (i,), dom=x * zn + to)

    def send_l(way, hop):
        owner = lists.at[up_z(way * (1 - hop))]
        return copy(owner, owner, sem_l, (way + 1, hop), **z_next[way])

    loop(1, zn, lambda i: send_ha(i).start())
    send_l(1, 1).start()
    send_l(-1, 1).start()
    for way, part in turns:
        send_z(way, 1, part).start()

    sub_id = lax.broadcasted_iota(jnp.int32, (verts, tall), 0).astype(F32)

    def chosen_rows(owner, d, part, sel_at, to_at):
        if part == 0:
            sel_at[...] = (sub_id == lists[owner, d % zn:d % zn + 1, :].astype(F32)).astype(BF16)
        to_at[...] = dot_t(sel_at[...], zrows[owner, part]).astype(BF16).reshape(xn, slots, cut)

    def pick(j, part):
        zz = up_z(j)
        chosen_rows(zz, -j, part, sel.at[zz], xsend.at[zz, part])
        arr[part, zz, x] = xsend[zz, part, x]
        for i in range(1, xn):
            to = lax.rem(x + i, xn)
            copy(xsend.at[zz, part, to], arr.at[part, zz, x], sem_x, (part,), dom=to * zn + z).start()

    def far_of(way):
        return range(xn // 2) if way > 0 else range(xn // 2, xn)

    def b_slot(way, step):
        return (way + 1) // 2 if step == 1 else 2

    def pick_beyond(way, step, part):
        side, slot = (way + 1) // 2, 3 * part + b_slot(way, step)
        owner = up_z(-way * hops)
        rows = bsend.at[side, step - 1, part]
        chosen_rows(owner, way * (hops + step), part, sel_b.at[side, step - 1], rows)
        for to in range(xn) if step == 1 else far_of(way):
            pltpu.make_async_remote_copy(
                src_ref=rows.at[to], dst_ref=arr.at[part, owner, x],
                send_sem=sem_b.at[0, slot, to], recv_sem=sem_b.at[1, slot, x],
                device_id={"dom": to * zn + up_z(way * step)}, device_id_type=pl.DeviceIdType.MESH,
            ).start()

    def hub_z():
        loop(1, zn, lambda i: send_ha(i).wait())
        for zz in range(zn):
            for q in range(quarter):
                hb_s[2 * zz:2 * zz + 2, q * lanes:(q + 1) * lanes] = ha[zz, 2 * q:2 * q + 2, :]
        hb[x] = hb_s[...]
        for i in range(1, xn):
            send_hb(i).start()

    def send_hb(i):
        return copy(hb_s, hb.at[x], sem_hb, (i,), dom=lax.rem(x + i, xn) * zn + z)

    block = hubtab.shape[1]

    lower, upper = pl.ds(0, block // 2), pl.ds(block // 2, block // 2)

    def y_peer(step):
        return {"group": up_y(step) * 2 + core}

    def send_y(i):
        if abs(i) in (1, 2):
            owner, to = y, i
        else:
            owner, to = (up_y(2), -(i == -3) or -2) if i <= 0 else (up_y(-2), i - 2)
        piece = hubtab.at[owner * 2 + core]
        if i in (0, 4):
            piece = piece.at[upper if i == 0 else lower]
        return copy(piece, piece, sem_y, (i % yn,), **y_peer(to))

    def send_sib(i):
        part = hubtab.at[up_y(-i) * 2 + core]
        return copy(part, part, sem_sib, (i,), **sibling)

    def hub_x():
        for i in range(1, xn):
            send_hb(i).wait()
        hubtab[group] = hb[...].reshape(block, width).astype(BF16)
        for i in (2, -2, 1, -1):
            send_y(i).start()
        send_sib(0).start()

    def hub_y():
        send_y(2).wait_recv()
        send_y(3).start()
        send_y(4).start()
        send_y(-2).wait_recv()
        send_y(-3).start()
        send_y(0).start()
        for i in (2, yn - 2):
            send_sib(i).start()
        for i in (1, -1):
            send_y(i).wait_recv()
            send_sib(i % yn).start()

    def hub_end():
        for i in (3, -3, 4):
            send_y(i).wait_recv()
            if i == 4:
                send_y(0).wait_recv()
            send_sib(i % yn).start()

    last = 2 * hops - 1
    hub_steps = [(min(1, last), hub_z), (min(3, last), hub_x), (max(last - 1, 1), hub_y)]
    for part in range(parts):
        pick(0, part)
    spot = 0
    for hop in range(1, hops + 1):
        for way in (1, -1):
            send_l(way, hop).wait_recv()
            if hop < hops:
                send_l(way, hop + 1).start()
        for part in range(parts):
            for way in (1, -1):
                send_z(way, hop, part).wait_recv()
                if hop < hops:
                    send_z(way, hop + 1, part).start()
                else:
                    pick_beyond(way, 1, part)
                    pick_beyond(way, 2, part)
            pick(-hop, part)
            pick(hop, part)
            if part in (parts // 2 - 1, parts - 1) and spot < last:
                for at, step in hub_steps:
                    if at == spot:
                        step()
                spot += 1
                tally_part(spot)
    for at, step in hub_steps:
        if at == spot:
            step()
    tally_part(spot + 1)
    hub_end()

    for load in loads[3:7]:
        load.wait()
    agg = dot_t(tab[0:verts, :], feat[...])
    pre = dot(feat[...], ws[...]) + bias[...]
    for i in range(yn):
        send_sib(i).wait()
    agg += dot_t(tab[hub_at:, :], hubtab[...].reshape(2 * yn * block, width))
    for part in range(parts):
        cols = slice(part * cut, (part + 1) * cut)
        if xn > 1:
            most = (pl.ds(0, 2 * hops + 1), pl.ds(0, xn - 1))
            whole = arr.at[part].at[most]
            copy(whole, whole, sem_x, (part,), dom=lax.rem(x + 1, xn) * zn + z).wait()
        for slot in range(3):
            for i in range(xn):
                copy(bsend.at[0, 0, part, 0], arr.at[part, 0, i], sem_b, (3 * part + slot, i), **sibling).wait()
        summed = agg[:, cols] + dot_t(tab[verts:hub_at, :], arr[part].reshape(near, cut))
        pre += dot((summed / fanout).astype(BF16), wn[cols, :])
    sigm = jax.nn.sigmoid(pre)
    outv[...] = (pre * sigm).astype(BF16)
    store = pltpu.make_async_copy(outv, out, sem_in.at[0])
    store.start()
    grad_pre = (cot[...].astype(F32) * sigm * (1.0 + pre * (1.0 - sigm))).astype(BF16)
    grad_mean = (dot_b(grad_pre, wn[...]) / fanout).astype(BF16)
    for part in range(parts):
        gm[part] = grad_mean[:, part * cut:(part + 1) * cut]

    def slot_grads(zz, part):
        rows = pl.ds(pl.multiple_of(verts + zz * tall, tall), tall)
        gsend[zz, part] = dot(tab[rows, :], gm[part]).astype(BF16).reshape(xn, slots, cut)

    def give_beyond(side, step, slot, to, part):
        way = 2 * side - 1
        return pltpu.make_async_remote_copy(
            src_ref=gsend.at[up_z(-way * (hops + step)), part, to], dst_ref=gback_b.at[side, step - 1, part, x],
            send_sem=sem_gb.at[0, 3 * part + slot, to], recv_sem=sem_gb.at[1, 3 * part + slot, x],
            device_id={"dom": to * zn + up_z(-way * step)}, device_id_type=pl.DeviceIdType.MESH,
        )

    my_side = 1 - x // (xn // 2)
    beyond = [(my_side, 2, 2), (1, 1, 1), (0, 1, 0)]

    def give(j, part):
        zz = up_z(j)
        slot_grads(zz, part)
        gback[zz, part, x] = gsend[zz, part, x]
        for i in range(1, xn):
            to = lax.rem(x + i, xn)
            copy(gsend.at[zz, part, to], gback.at[zz, part, x], sem_xg, (j * parts + part,), dom=to * zn + z).start()

    def give_first(part):
        for side, step, slot in beyond:
            slot_grads(up_z((1 - 2 * side) * (hops + step)), part)
            for to in range(xn):
                give_beyond(side, step, slot, to, part).start()
        give(hops, part)
        give(zn - hops, part)

    give_first(0)
    gback_b[1, 1, :, xn // 2:] = jnp.zeros((parts, xn // 2, slots, cut), BF16)
    gback_b[0, 1, :, :xn // 2] = jnp.zeros((parts, xn // 2, slots, cut), BF16)

    def send_sibg(owner):
        return copy(sib_s.at[owner], sib.at[owner], sem_sibg, (owner,), **sibling)

    def hub_terms(owner):
        rows = pl.ds(pl.multiple_of(hub_at + owner * 2 * block, 32), 2 * block)
        hubg[pl.ds(2 * owner, 2)] = dot(tab[rows, :], grad_mean).reshape(2, block, width)
        sib_s[owner] = hubg[2 * owner + 1 - core].astype(BF16)
        send_sibg(owner).start()

    loop(0, yn, hub_terms)

    for part in range(1, parts):
        give_first(part)

    def give_rest(t):
        j = lax.rem(jnp.where(lax.rem(t, 2) == 1, half_z - (t + 1) // 2, t // 2 - half_z) + zn, zn)
        for part in range(parts):
            give(j, part)

    loop(5, zn, give_rest)

    def given(j, part):
        some = pl.ds(0, xn - 1)
        zz = up_z(j)
        at = (j % zn) * parts + part
        return copy(gsend.at[zz, part, some], gback.at[zz, part, some], sem_xg, (at,), dom=lax.rem(x + 1, xn) * zn + z)

    def owed(j, part):
        if xn > 1:
            given(j, part).wait_recv()
        zz = up_z(j)
        value = dot(sel[zz], gback[zz, part].reshape(tall, cut))
        if abs(j) == hops:
            way = 1 if j < 0 else -1
            side = (way + 1) // 2
            for step in (1, 2):
                slot = 3 * part + b_slot(way, step)
                for i in range(xn) if step == 1 else far_of(way):
                    copy(gsend.at[0, part, 0], gback_b.at[side, step - 1, part, i], sem_gb, (slot, i), **sibling).wait_recv()
                value += dot(sel_b[side, step - 1], gback_b[side, step - 1, part].reshape(tall, cut))
        return value

    def send_g(way, hop, part):
        at = ((way + 1) // 2, hop, part)
        return copy(zout.at[at], zin.at[at], sem_rz, (way + 1, hop, part), **z_next[way])

    def step_z(hop):
        for way, part in turns:
            at = (way + 1) // 2
            value = owed(way * hop, part)
            if hop < hops:
                send_g(way, hop + 1, part).wait_recv()
                value = value + zin[at, hop + 1, part].astype(F32)
            zout[at, hop, part] = value.astype(BF16)
            send_g(way, hop, part).start()

    def mine(owner):
        return hubg[owner * 2 + core] + sib[owner].astype(F32)

    reach = (1, -1, 2, -2, 1, -1, 2, -2)

    def send_yg(i):
        src, dst = yg_s.at[i], yg.at[i]
        if i in (2, 3):
            rows = lower if i == 2 else upper
            src, dst = src.at[rows], dst.at[rows]
        return copy(src, dst, sem_yg, (i,), **y_peer(reach[i]))

    def start_y():
        loop(0, yn, lambda i: send_sibg(i).wait_recv())
        for i, owner in enumerate((3, -3, 4, -4, 1, -1)):
            yg_s[i] = mine(up_y(owner)).astype(BF16)
            send_yg(i).start()

    def relay_y():
        for i in (0, 1):
            send_yg(i).wait_recv()
            send_yg(i + 2).wait_recv()
            value = mine(up_y(reach[i + 6])) + yg[i].astype(F32)
            for at, some in ((0, slice(0, block // 2)), (1, slice(block // 2, block))):
                term = value[some]
                if at == i:
                    term = term + yg[i + 2, some].astype(F32)
                yg_s[i + 6, some] = term.astype(BF16)
            send_yg(i + 6).start()

    def send_xb(i):
        to = lax.rem(x + i, xn)
        return copy(xb_s.at[to], xb.at[i], sem_xb, (i,), dom=to * zn + z)

    def send_za(i):
        to = up_z(i)
        return copy(za_s.at[to], za.at[i], sem_za, (i,), dom=x * zn + to)

    def start_x():
        total = mine(y)
        for i in range(4, 8):
            send_yg(i).wait_recv()
            total = total + yg[i].astype(F32)
        xb_s[...] = total.reshape(xn, 2 * zn, width)
        for i in range(1, xn):
            send_xb(i).start()

    def end_x():
        total = xb_s[x]
        for i in range(1, xn):
            send_xb(i).wait_recv()
            total = total + xb[i]
        for zz in range(zn):
            for q in range(quarter):
                za_s[zz, 2 * q:2 * q + 2, :] = total[2 * zz:2 * zz + 2, q * lanes:(q + 1) * lanes]
        loop(1, zn, lambda i: send_za(i).start())

    def self_part():
        gout[...] = dot(tab[0:verts, :], grad_mean) + dot_b(grad_pre, ws[...])

    def wait_sent():
        for hop in range(1, hops + 1):
            for way, part in turns:
                send_z(way, hop, part).wait_send()
            send_l(1, hop).wait_send()
            send_l(-1, hop).wait_send()
        for i in (1, -1, 2, -2, 3, -3, 4, 0):
            send_y(i).wait_send()
        store.wait()

    def wait_given():
        for hop in range(2, hops + 1):
            for way, part in turns:
                send_g(way, hop, part).wait_send()
        for i in range(8):
            send_yg(i).wait_send()
        for i in range(yn):
            send_sibg(i).wait_send()
        for part in range(parts):
            if xn > 1:
                for j in range(zn):
                    if min(j, zn - j) <= hops:
                        given(j, part).wait_send()
            for side, step, slot in beyond:
                for to in range(xn):
                    give_beyond(side, step, slot, to, part).wait_send()

    jobs = [(hops, self_part), (hops, wait_sent), (hops, relay_y), (min(2, hops), start_x), (1, end_x), (1, wait_given)]
    start_y()
    for hop in range(hops, 0, -1):
        step_z(hop)
        for at, job in jobs:
            if at == hop:
                job()
    for part in range(parts):
        cols = slice(part * cut, (part + 1) * cut)
        gout[:, cols] += owed(0, part)
    for way, part in turns:
        cols = slice(part * cut, (part + 1) * cut)
        send_g(way, 1, part).wait_recv()
        gout[:, cols] += zin[(way + 1) // 2, 1, part].astype(F32)
    loop(1, zn, lambda i: send_za(i).wait_recv())
    hub_sum = za_s[z]
    for i in range(1, zn):
        hub_sum = hub_sum + za[i]
    rows_of = lax.broadcasted_iota(jnp.int32, (verts, lanes), 0)
    for q in range(quarter):
        cols = slice(q * lanes, (q + 1) * lanes)
        gout[:, cols] += jnp.where(rows_of == hub0, hub_sum[2 * q:2 * q + 1], 0.0) + jnp.where(
            rows_of == hub1, hub_sum[2 * q + 1:2 * q + 2], 0.0
        )

    for way, part in turns:
        send_g(way, 1, part).wait_send()
    for i in range(1, xn):
        send_xb(i).wait_send()
    loop(1, zn, lambda i: send_za(i).wait_send())


def body(features, cotangent, w_self, w_neigh, bias, neighbours, send_rows, hub_local):
    verts, width = features.shape
    peers, slots = send_rows.shape[1:]
    xn, zn = peers // ZN, ZN
    groups = lax.axis_size("group")
    yn = groups // 2
    half_z, parts = zn // 2, PARTS
    near = peers * slots
    tall = xn * slots
    block = 2 * peers
    tile = width // 64
    cut = width // parts
    vmem = pl.BlockSpec(memory_space=pltpu.VMEM)
    dma = pltpu.SemaphoreType.DMA
    edge = (zn, parts, xn, slots, cut)
    hub = (yn, block, width)
    return pl.pallas_call(
        functools.partial(kernel, yn, xn, zn),
        out_shape=(
            jax.ShapeDtypeStruct((verts, width), BF16),
            jax.ShapeDtypeStruct((verts, width), F32),
        ),
        in_specs=[pl.BlockSpec(memory_space=pl.ANY)] * 7 + [pl.BlockSpec(memory_space=pltpu.SMEM)],
        out_specs=(pl.BlockSpec(memory_space=pl.ANY), vmem),
        scratch_shapes=[
            pltpu.VMEM((verts, width), BF16),
            pltpu.VMEM((verts, width), BF16),
            pltpu.VMEM((width, width), BF16),
            pltpu.VMEM((width, width), BF16),
            pltpu.VMEM((1, width), F32),
            pltpu.VMEM(neighbours.shape[::-1], jnp.int32),
            pltpu.VMEM((slots, peers), jnp.int32),
            pltpu.VMEM((zn, tall), F32),
            pltpu.VMEM((verts, width), BF16),
            pltpu.VMEM((parts, verts, cut), BF16),
            pltpu.VMEM((verts + near + groups * block, verts), BF16),
            pltpu.VMEM((zn, verts, tall), BF16),
            pltpu.VMEM((2, 2, verts, tall), BF16),
            pltpu.VMEM((16, tall), F32),
            pltpu.VMEM((zn, 16, tall), BF16),
            pltpu.VMEM((zn, parts, verts, cut), BF16),
            pltpu.VMEM(edge, BF16),
            pltpu.VMEM((2, 2) + edge[1:], BF16),
            pltpu.VMEM((parts, zn, xn, slots, cut), BF16),
            pltpu.VMEM(edge, BF16),
            pltpu.VMEM(edge, BF16),
            pltpu.VMEM((2, 2) + edge[1:], BF16),
            pltpu.VMEM((2, half_z - 1, parts, verts, cut), BF16),
            pltpu.VMEM((2, half_z - 1, parts, verts, cut), BF16),
            pltpu.VMEM((groups, block, width), BF16),
            pltpu.VMEM((tile, 128), F32),
            pltpu.VMEM((zn, tile, 128), F32),
            pltpu.VMEM((2 * zn, width), F32),
            pltpu.VMEM((xn, 2 * zn, width), F32),
            pltpu.VMEM((groups, block, width), F32),
            pltpu.VMEM(hub, BF16),
            pltpu.VMEM(hub, BF16),
            pltpu.VMEM(hub, BF16),
            pltpu.VMEM(hub, BF16),
            pltpu.VMEM((xn, 2 * zn, width), F32),
            pltpu.VMEM((xn, 2 * zn, width), F32),
            pltpu.VMEM((zn, tile, 128), F32),
            pltpu.VMEM((zn, tile, 128), F32),
            dma((2, 3, half_z, parts)),
            dma((2, 3, half_z, parts)),
            dma((2, 3, half_z)),
            dma((2, parts)),
            dma((2, 3 * parts, xn)),
            dma((2, zn * parts)),
            dma((2, 3 * parts, xn)),
            dma((2, zn)),
            dma((2, xn)),
            dma((2, yn)),
            dma((2, yn)),
            dma((2, yn)),
            dma((2, yn)),
            dma((2, xn)),
            dma((2, zn)),
            dma((7 + parts,)),
        ],
        compiler_params=pltpu.CompilerParams(
            collective_id=0, has_side_effects=True, vmem_limit_bytes=60 * 1024 * 1024
        ),
    )(features, cotangent, w_self, w_neigh, bias.reshape(1, width), neighbours.T, send_rows.reshape(peers, slots).T, hub_local)


def solution(mesh):
    rows = P(("group", "dom"), None)
    return jax.shard_map(
        body,
        mesh=mesh,
        in_specs=(rows, rows, P(), P(), P(), rows, P(("group", "dom"), None, None), P(("group", "dom"))),
        out_specs=(rows, rows),
        check_vma=False,
    )
```

```python
import functools

import jax
import jax.numpy as jnp
from jax import lax
from jax.experimental import pallas as pl
from jax.experimental.pallas import tpu as pltpu
from jax.sharding import PartitionSpec as P

ZN = 12
PARTS = 2
F32 = jnp.float32
BF16 = jnp.bfloat16


def dot(left, right):
    return jnp.dot(left, right, preferred_element_type=F32)


def kernel(
    yn, xn, zn, feat_in, cot_in, ws_in, wn_in, bias_in, nbrt_in, sr_in, hubl, out, gout,
    feat, cot, ws, wn, bias, nbrt, sr, lst, gm,
    tab, tabn, selt, wnt, wst, sel, sel_b, rel, lists, zrows, xsend, bsend, arr, gsend, gback, gback_b, zout, zin, hubtab,
    ha_s, ha, hb_s, hb, hubg, sib_s, sib, yg_s, yg, xb_s, xb, za_s, za,
    sem_z, sem_rz, sem_l, sem_x, sem_b, sem_xg, sem_gb, sem_ha, sem_hb, sem_y, sem_sib, sem_sibg, sem_yg, sem_xb, sem_za, sem_in,
):
    verts, width = feat.shape
    fanout = nbrt.shape[0]
    slots = arr.shape[3]
    lanes = 128
    tall = xn * slots
    quarter = width // lanes
    near = zn * tall
    hub_at = verts + near
    group = lax.axis_index("group")
    dom = lax.axis_index("dom")
    y, core = group // 2, lax.rem(group, 2)
    x, z = dom // zn, lax.rem(dom, zn)
    half_z = zn // 2
    hops = half_z - 2
    parts = sem_z.shape[3]
    cut = width // parts

    def up_y(step):
        return lax.rem(y + step + 2 * yn, yn)

    def up_z(step):
        return lax.rem(z + step + 2 * zn, zn)

    def copy(src, dst, sems, at, **to):
        return pltpu.make_async_remote_copy(
            src_ref=src, dst_ref=dst, send_sem=sems.at[(0,) + at], recv_sem=sems.at[(1,) + at],
            device_id=to, device_id_type=pl.DeviceIdType.MESH,
        )

    def loop(lo, hi, body):
        lax.fori_loop(lo, hi, lambda i, c: (body(i), c)[1], 0)

    z_next = {1: {"dom": x * zn + up_z(1)}, -1: {"dom": x * zn + up_z(-1)}}
    sibling = {"group": y * 2 + 1 - core}

    barrier = pltpu.get_barrier_semaphore()

    def greet(**to):
        pl.semaphore_signal(barrier, 1, device_id=to, device_id_type=pl.DeviceIdType.MESH)

    loop(1, zn, lambda i: greet(dom=x * zn + up_z(i)))
    for i in range(1, xn):
        greet(dom=lax.rem(x + i, xn) * zn + z)
        for step in (-2, -1, 1, 2):
            greet(dom=lax.rem(x + i, xn) * zn + up_z(step))
    for step in (-2, -1, 1, 2):
        greet(group=up_y(step) * 2 + core)
    greet(**sibling)

    sources = (feat_in, sr_in, nbrt_in, cot_in, ws_in, wn_in, bias_in)
    loads = [
        pltpu.make_async_copy(src, dst, sem_in.at[i])
        for i, (src, dst) in enumerate(zip(sources, (feat, sr, nbrt, cot, ws, wn, bias)))
    ]
    for part in range(parts):
        cols = feat_in.at[:, pl.ds(part * cut, cut)]
        loads.append(pltpu.make_async_copy(cols, zrows.at[z, part], sem_in.at[7 + part]))
    for i in (0, 1, 7, 2, 3, 4, 5, 6):
        loads[i].start()
    for load in loads[8:]:
        load.start()
    loads[0].wait()

    row_id = lax.broadcasted_iota(jnp.int32, (16, verts), 0)
    vert_id = lax.broadcasted_iota(jnp.int32, (16, verts), 1)
    hub0, hub1 = hubl[0], hubl[1]
    wanted = jnp.where(row_id == 0, hub0, jnp.where(row_id == 1, hub1, -1))
    hub_rows = dot((vert_id == wanted).astype(BF16), feat[...])
    for q in range(quarter):
        ha_s[2 * q:2 * q + 2, :] = hub_rows[0:2, q * lanes:(q + 1) * lanes]
    ha[z] = ha_s[...]
    loads[1].wait()
    by_peer = sr[...].astype(F32).T
    for xx in range(xn):
        lst[:, xx * slots:(xx + 1) * slots] = by_peer[xx * zn:(xx + 1) * zn, :]
    rel[...] = jnp.full_like(rel, -1.0)
    for d in range(zn):
        rel[d:d + 1, :] = lst[pl.ds(up_z(d), 1), :]
    lists[z] = rel[...].astype(BF16)

    def tally(i):
        sub = lax.broadcasted_iota(jnp.int32, (tall, verts), 0)
        at = i * tall
        zz = i - verts // tall
        border = verts + zz * slots + (sub // slots) * (zn * slots) + lax.rem(sub, slots)
        is_border = jnp.logical_and(zz >= 0, zz < zn)
        rows = jnp.where(is_border, border, at + sub)
        total = jnp.zeros((tall, verts), F32)
        for e in range(fanout):
            total = jnp.where(nbrt[e:e + 1, :] == rows, total + 1.0, total)
        tab[pl.ds(pl.multiple_of(at, tall), tall), :] = total.astype(BF16)
        tabn[i] = total.T.astype(BF16)

    tiles = tab.shape[0] // tall
    spots = 2 * hops + 1
    cuts = [tiles * k // spots for k in range(spots + 1)]

    def tally_part(k):
        loop(cuts[k], cuts[k + 1], tally)

    loads[2].wait()
    tally_part(0)
    for load in loads[7:]:
        load.wait()
    pl.semaphore_wait(barrier, zn - 1 + 5 * (xn - 1) + 5)

    def send_z(way, hop, part):
        piece = zrows.at[up_z(way * (1 - hop)), part]
        return copy(piece, piece, sem_z, (way + 1, hop, part), **z_next[way])

    turns = [(way, part) for part in range(parts) for way in (1, -1)]

    def send_ha(i):
        to = up_z(i)
        return copy(ha_s, ha.at[z], sem_ha, (i,), dom=x * zn + to)

    def send_l(way, hop):
        owner = lists.at[up_z(way * (1 - hop))]
        return copy(owner, owner, sem_l, (way + 1, hop), **z_next[way])

    loop(1, zn, lambda i: send_ha(i).start())
    send_l(1, 1).start()
    send_l(-1, 1).start()
    for way, part in turns:
        send_z(way, 1, part).start()

    sub_id = lax.broadcasted_iota(jnp.int32, (verts, tall), 0).astype(F32)

    def wanted_by(owner, d, sel_at, row):
        chosen = (sub_id == lists[owner, d % zn:d % zn + 1, :].astype(F32)).astype(F32)
        sel_at[...] = chosen.astype(BF16)
        selt[row] = chosen.T.astype(BF16)

    def prepare(way, hop):
        side, owner = (way + 1) // 2, up_z(-way * hop)
        wanted_by(owner, way * hop, sel.at[owner], 3 * side)
        if hop == hops:
            for step in (1, 2):
                wanted_by(owner, way * (hop + step), sel_b.at[side, step - 1], 3 * side + step)

    def pick(way, hop, part):
        side, zz = (way + 1) // 2, up_z(-way * hop)
        if hop == hops:
            rows = dot(selt[3 * side:3 * side + 3].reshape(3 * tall, verts), zrows[zz, part]).astype(BF16)
            for step in (1, 2):
                bsend[side, step - 1, part] = rows[step * tall:(step + 1) * tall].reshape(xn, slots, cut)
                send_beyond(way, step, part)
            rows = rows[:tall]
        else:
            rows = dot(selt[3 * side], zrows[zz, part]).astype(BF16)
        xsend[zz, part] = rows.reshape(xn, slots, cut)
        arr[part, zz, x] = xsend[zz, part, x]
        for i in range(1, xn):
            to = lax.rem(x + i, xn)
            copy(xsend.at[zz, part, to], arr.at[part, zz, x], sem_x, (part,), dom=to * zn + z).start()

    def far_of(way):
        return range(xn // 2) if way > 0 else range(xn // 2, xn)

    def b_slot(way, step):
        return (way + 1) // 2 if step == 1 else 2

    def send_beyond(way, step, part):
        side, slot = (way + 1) // 2, 3 * part + b_slot(way, step)
        for to in range(xn) if step == 1 else far_of(way):
            pltpu.make_async_remote_copy(
                src_ref=bsend.at[side, step - 1, part, to], dst_ref=arr.at[part, up_z(-way * hops), x],
                send_sem=sem_b.at[0, slot, to], recv_sem=sem_b.at[1, slot, x],
                device_id={"dom": to * zn + up_z(way * step)}, device_id_type=pl.DeviceIdType.MESH,
            ).start()

    def hub_z():
        loop(1, zn, lambda i: send_ha(i).wait())
        for zz in range(zn):
            for q in range(quarter):
                hb_s[2 * zz:2 * zz + 2, q * lanes:(q + 1) * lanes] = ha[zz, 2 * q:2 * q + 2, :]
        hb[x] = hb_s[...]
        for i in range(1, xn):
            send_hb(i).start()

    def send_hb(i):
        return copy(hb_s, hb.at[x], sem_hb, (i,), dom=lax.rem(x + i, xn) * zn + z)

    block = hubtab.shape[1]

    lower, upper = pl.ds(0, block // 2), pl.ds(block // 2, block // 2)

    def y_peer(step):
        return {"group": up_y(step) * 2 + core}

    def send_y(i):
        if abs(i) in (1, 2):
            owner, to = y, i
        else:
            owner, to = (up_y(2), -(i == -3) or -2) if i <= 0 else (up_y(-2), i - 2)
        piece = hubtab.at[owner * 2 + core]
        if i in (0, 4):
            piece = piece.at[upper if i == 0 else lower]
        return copy(piece, piece, sem_y, (i % yn,), **y_peer(to))

    def send_sib(i):
        part = hubtab.at[up_y(-i) * 2 + core]
        return copy(part, part, sem_sib, (i,), **sibling)

    def hub_x():
        for i in range(1, xn):
            send_hb(i).wait()
        hubtab[group] = hb[...].reshape(block, width).astype(BF16)
        for i in (2, -2, 1, -1):
            send_y(i).start()
        send_sib(0).start()

    def hub_y():
        send_y(2).wait_recv()
        send_y(3).start()
        send_y(4).start()
        send_y(-2).wait_recv()
        send_y(-3).start()
        send_y(0).start()
        for i in (2, yn - 2):
            send_sib(i).start()
        for i in (1, -1):
            send_y(i).wait_recv()
            send_sib(i % yn).start()

    def hub_end():
        for i in (3, -3, 4):
            send_y(i).wait_recv()
            if i == 4:
                send_y(0).wait_recv()
            send_sib(i % yn).start()

    last = 2 * hops - 1
    hub_steps = [(min(1, last), hub_z), (min(3, last), hub_x), (max(last - 1, 1), hub_y)]
    prepare(1, 0)
    for part in range(parts):
        pick(1, 0, part)
    spot = 0
    for hop in range(1, hops + 1):
        for way in (1, -1):
            send_l(way, hop).wait_recv()
            if hop < hops:
                send_l(way, hop + 1).start()
            prepare(way, hop)
        for part in range(parts):
            for way in (1, -1):
                send_z(way, hop, part).wait_recv()
                if hop < hops:
                    send_z(way, hop + 1, part).start()
                else:
                    pick(way, hop, part)
            if hop < hops:
                pick(1, hop, part)
                pick(-1, hop, part)
            if part in (parts // 2 - 1, parts - 1) and spot < last:
                for at, step in hub_steps:
                    if at == spot:
                        step()
                spot += 1
                tally_part(spot)
    for at, step in hub_steps:
        if at == spot:
            step()
    tally_part(spot + 1)
    hub_end()

    def counts(lo, hi):
        return jnp.concatenate([tabn[i] for i in range(lo // tall, hi // tall)], axis=1)

    for load in loads[3:7]:
        load.wait()
    wnt[...] = wn[...].T
    wst[...] = ws[...].T
    agg = dot(counts(0, verts), feat[...])
    pre = dot(feat[...], ws[...]) + bias[...]
    for i in range(yn):
        send_sib(i).wait()
    agg += dot(counts(hub_at, tab.shape[0]), hubtab[...].reshape(2 * yn * block, width))
    for part in range(parts):
        cols = slice(part * cut, (part + 1) * cut)
        if xn > 1:
            most = (pl.ds(0, 2 * hops + 1), pl.ds(0, xn - 1))
            whole = arr.at[part].at[most]
            copy(whole, whole, sem_x, (part,), dom=lax.rem(x + 1, xn) * zn + z).wait()
        for slot in range(3):
            for i in range(xn):
                copy(bsend.at[0, 0, part, 0], arr.at[part, 0, i], sem_b, (3 * part + slot, i), **sibling).wait()
        summed = agg[:, cols] + dot(counts(verts, hub_at), arr[part].reshape(near, cut))
        pre += dot((summed / fanout).astype(BF16), wn[cols, :])
    sigm = jax.nn.sigmoid(pre)
    grad_pre = (cot[...].astype(F32) * sigm * (1.0 + pre * (1.0 - sigm))).astype(BF16)
    grad_mean = (dot(grad_pre, wnt[...]) / fanout).astype(BF16)
    for part in range(parts):
        gm[part] = grad_mean[:, part * cut:(part + 1) * cut]
    out[...] = (pre * sigm).astype(BF16)

    def slot_grads(zz, part):
        rows = pl.ds(pl.multiple_of(verts + zz * tall, tall), tall)
        gsend[zz, part] = dot(tab[rows, :], gm[part]).astype(BF16).reshape(xn, slots, cut)

    def give_beyond(side, step, slot, to, part):
        way = 2 * side - 1
        return pltpu.make_async_remote_copy(
            src_ref=gsend.at[up_z(-way * (hops + step)), part, to], dst_ref=gback_b.at[side, step - 1, part, x],
            send_sem=sem_gb.at[0, 3 * part + slot, to], recv_sem=sem_gb.at[1, 3 * part + slot, x],
            device_id={"dom": to * zn + up_z(-way * step)}, device_id_type=pl.DeviceIdType.MESH,
        )

    my_side = 1 - x // (xn // 2)
    beyond = [(my_side, 2, 2), (1, 1, 1), (0, 1, 0)]

    def give(j, part):
        zz = up_z(j)
        slot_grads(zz, part)
        gback[zz, part, x] = gsend[zz, part, x]
        for i in range(1, xn):
            to = lax.rem(x + i, xn)
            copy(gsend.at[zz, part, to], gback.at[zz, part, x], sem_xg, (j * parts + part,), dom=to * zn + z).start()

    def give_first(part):
        for side, step, slot in beyond:
            slot_grads(up_z((1 - 2 * side) * (hops + step)), part)
            for to in range(xn):
                give_beyond(side, step, slot, to, part).start()
        give(hops, part)
        give(zn - hops, part)

    give_first(0)
    gback_b[1, 1, :, xn // 2:] = jnp.zeros((parts, xn // 2, slots, cut), BF16)
    gback_b[0, 1, :, :xn // 2] = jnp.zeros((parts, xn // 2, slots, cut), BF16)

    def send_sibg(owner):
        return copy(sib_s.at[owner], sib.at[owner], sem_sibg, (owner,), **sibling)

    def hub_terms(owner):
        rows = pl.ds(pl.multiple_of(hub_at + owner * 2 * block, 32), 2 * block)
        hubg[pl.ds(2 * owner, 2)] = dot(tab[rows, :], grad_mean).reshape(2, block, width)
        sib_s[owner] = hubg[2 * owner + 1 - core].astype(BF16)
        send_sibg(owner).start()

    loop(0, yn, hub_terms)

    for part in range(1, parts):
        give_first(part)

    def give_rest(t):
        j = lax.rem(jnp.where(lax.rem(t, 2) == 1, half_z - (t + 1) // 2, t // 2 - half_z) + zn, zn)
        for part in range(parts):
            give(j, part)

    loop(5, zn, give_rest)

    def given(j, part):
        some = pl.ds(0, xn - 1)
        zz = up_z(j)
        at = (j % zn) * parts + part
        return copy(gsend.at[zz, part, some], gback.at[zz, part, some], sem_xg, (at,), dom=lax.rem(x + 1, xn) * zn + z)

    def owed(j, part):
        if xn > 1:
            given(j, part).wait_recv()
        zz = up_z(j)
        value = dot(sel[zz], gback[zz, part].reshape(tall, cut))
        if abs(j) == hops:
            way = 1 if j < 0 else -1
            side = (way + 1) // 2
            for step in (1, 2):
                slot = 3 * part + b_slot(way, step)
                for i in range(xn) if step == 1 else far_of(way):
                    copy(gsend.at[0, part, 0], gback_b.at[side, step - 1, part, i], sem_gb, (slot, i), **sibling).wait_recv()
                value += dot(sel_b[side, step - 1], gback_b[side, step - 1, part].reshape(tall, cut))
        return value

    def send_g(way, hop, part):
        at = ((way + 1) // 2, hop, part)
        return copy(zout.at[at], zin.at[at], sem_rz, (way + 1, hop, part), **z_next[way])

    def step_z(hop, part):
        for way in (1, -1):
            at = (way + 1) // 2
            value = owed(way * hop, part)
            if hop < hops:
                send_g(way, hop + 1, part).wait_recv()
                value = value + zin[at, hop + 1, part].astype(F32)
            zout[at, hop, part] = value.astype(BF16)
            send_g(way, hop, part).start()

    def mine(owner):
        return hubg[owner * 2 + core] + sib[owner].astype(F32)

    reach = (1, -1, 2, -2, 1, -1, 2, -2)

    def send_yg(i):
        src, dst = yg_s.at[i], yg.at[i]
        if i in (2, 3):
            rows = lower if i == 2 else upper
            src, dst = src.at[rows], dst.at[rows]
        return copy(src, dst, sem_yg, (i,), **y_peer(reach[i]))

    def start_y():
        loop(0, yn, lambda i: send_sibg(i).wait_recv())
        for i, owner in enumerate((3, -3, 4, -4, 1, -1)):
            yg_s[i] = mine(up_y(owner)).astype(BF16)
            send_yg(i).start()

    def relay_y():
        for i in (0, 1):
            send_yg(i).wait_recv()
            send_yg(i + 2).wait_recv()
            value = mine(up_y(reach[i + 6])) + yg[i].astype(F32)
            for at, some in ((0, slice(0, block // 2)), (1, slice(block // 2, block))):
                term = value[some]
                if at == i:
                    term = term + yg[i + 2, some].astype(F32)
                yg_s[i + 6, some] = term.astype(BF16)
            send_yg(i + 6).start()

    def send_xb(i):
        to = lax.rem(x + i, xn)
        return copy(xb_s.at[to], xb.at[i], sem_xb, (i,), dom=to * zn + z)

    def send_za(i):
        to = up_z(i)
        return copy(za_s.at[to], za.at[i], sem_za, (i,), dom=x * zn + to)

    def start_x():
        total = mine(y)
        for i in range(4, 8):
            send_yg(i).wait_recv()
            total = total + yg[i].astype(F32)
        xb_s[...] = total.reshape(xn, 2 * zn, width)
        for i in range(1, xn):
            send_xb(i).start()

    def end_x():
        total = xb_s[x]
        for i in range(1, xn):
            send_xb(i).wait_recv()
            total = total + xb[i]
        for zz in range(zn):
            for q in range(quarter):
                za_s[zz, 2 * q:2 * q + 2, :] = total[2 * zz:2 * zz + 2, q * lanes:(q + 1) * lanes]
        loop(1, zn, lambda i: send_za(i).start())

    def self_part():
        gout[...] = dot(tab[0:verts, :], grad_mean) + dot(grad_pre, wst[...])

    def wait_sent():
        for hop in range(1, hops + 1):
            for way, part in turns:
                send_z(way, hop, part).wait_send()
            send_l(1, hop).wait_send()
            send_l(-1, hop).wait_send()
        for i in (1, -1, 2, -2, 3, -3, 4, 0):
            send_y(i).wait_send()

    def wait_given():
        for hop in range(2, hops + 1):
            for way, part in turns:
                send_g(way, hop, part).wait_send()
        for i in range(8):
            send_yg(i).wait_send()
        for i in range(yn):
            send_sibg(i).wait_send()
        for part in range(parts):
            if xn > 1:
                for j in range(zn):
                    if min(j, zn - j) <= hops:
                        given(j, part).wait_send()
            for side, step, slot in beyond:
                for to in range(xn):
                    give_beyond(side, step, slot, to, part).wait_send()

    end = parts - 1
    jobs = [
        (hops, 0, self_part), (hops, end, wait_sent), (hops - 1, 0, relay_y),
        (min(2, hops), 0, start_x) if hops > 1 else (1, end, start_x),
        (1, 0, end_x) if hops > 1 else (1, end, end_x), (1, end, wait_given),
    ]
    start_y()
    for hop in range(hops, 0, -1):
        for part in range(parts):
            step_z(hop, part)
            for at, when, job in jobs:
                if (at, when) == (hop, part):
                    job()
    for part in range(parts):
        cols = slice(part * cut, (part + 1) * cut)
        gout[:, cols] += owed(0, part)
    for way, part in turns:
        cols = slice(part * cut, (part + 1) * cut)
        send_g(way, 1, part).wait_recv()
        gout[:, cols] += zin[(way + 1) // 2, 1, part].astype(F32)
    loop(1, zn, lambda i: send_za(i).wait_recv())
    hub_sum = za_s[z]
    for i in range(1, zn):
        hub_sum = hub_sum + za[i]
    rows_of = lax.broadcasted_iota(jnp.int32, (verts, lanes), 0)
    for q in range(quarter):
        cols = slice(q * lanes, (q + 1) * lanes)
        gout[:, cols] += jnp.where(rows_of == hub0, hub_sum[2 * q:2 * q + 1], 0.0) + jnp.where(
            rows_of == hub1, hub_sum[2 * q + 1:2 * q + 2], 0.0
        )

    for way, part in turns:
        send_g(way, 1, part).wait_send()
    for i in range(1, xn):
        send_xb(i).wait_send()
    loop(1, zn, lambda i: send_za(i).wait_send())


def body(features, cotangent, w_self, w_neigh, bias, neighbours, send_rows, hub_local):
    verts, width = features.shape
    peers, slots = send_rows.shape[1:]
    xn, zn = peers // ZN, ZN
    groups = lax.axis_size("group")
    yn = groups // 2
    half_z, parts = zn // 2, PARTS
    near = peers * slots
    tall = xn * slots
    block = 2 * peers
    tile = width // 64
    cut = width // parts
    vmem = pl.BlockSpec(memory_space=pltpu.VMEM)
    dma = pltpu.SemaphoreType.DMA
    edge = (zn, parts, xn, slots, cut)
    hub = (yn, block, width)
    return pl.pallas_call(
        functools.partial(kernel, yn, xn, zn),
        out_shape=(
            pltpu.VMEM((verts, width), BF16),
            pltpu.VMEM((verts, width), F32),
        ),
        in_specs=[pl.BlockSpec(memory_space=pl.ANY)] * 7 + [pl.BlockSpec(memory_space=pltpu.SMEM)],
        out_specs=(vmem, vmem),
        scratch_shapes=[
            pltpu.VMEM((verts, width), BF16),
            pltpu.VMEM((verts, width), BF16),
            pltpu.VMEM((width, width), BF16),
            pltpu.VMEM((width, width), BF16),
            pltpu.VMEM((1, width), F32),
            pltpu.VMEM(neighbours.shape[::-1], jnp.int32),
            pltpu.VMEM((slots, peers), jnp.int32),
            pltpu.VMEM((zn, tall), F32),
            pltpu.VMEM((parts, verts, cut), BF16),
            pltpu.VMEM((verts + near + groups * block, verts), BF16),
            pltpu.VMEM(((verts + near + groups * block) // tall, verts, tall), BF16),
            pltpu.VMEM((6, tall, verts), BF16),
            pltpu.VMEM((width, width), BF16),
            pltpu.VMEM((width, width), BF16),
            pltpu.VMEM((zn, verts, tall), BF16),
            pltpu.VMEM((2, 2, verts, tall), BF16),
            pltpu.VMEM((16, tall), F32),
            pltpu.VMEM((zn, 16, tall), BF16),
            pltpu.VMEM((zn, parts, verts, cut), BF16),
            pltpu.VMEM(edge, BF16),
            pltpu.VMEM((2, 2) + edge[1:], BF16),
            pltpu.VMEM((parts, zn, xn, slots, cut), BF16),
            pltpu.VMEM(edge, BF16),
            pltpu.VMEM(edge, BF16),
            pltpu.VMEM((2, 2) + edge[1:], BF16),
            pltpu.VMEM((2, half_z - 1, parts, verts, cut), BF16),
            pltpu.VMEM((2, half_z - 1, parts, verts, cut), BF16),
            pltpu.VMEM((groups, block, width), BF16),
            pltpu.VMEM((tile, 128), F32),
            pltpu.VMEM((zn, tile, 128), F32),
            pltpu.VMEM((2 * zn, width), F32),
            pltpu.VMEM((xn, 2 * zn, width), F32),
            pltpu.VMEM((groups, block, width), F32),
            pltpu.VMEM(hub, BF16),
            pltpu.VMEM(hub, BF16),
            pltpu.VMEM(hub, BF16),
            pltpu.VMEM(hub, BF16),
            pltpu.VMEM((xn, 2 * zn, width), F32),
            pltpu.VMEM((xn, 2 * zn, width), F32),
            pltpu.VMEM((zn, tile, 128), F32),
            pltpu.VMEM((zn, tile, 128), F32),
            dma((2, 3, half_z, parts)),
            dma((2, 3, half_z, parts)),
            dma((2, 3, half_z)),
            dma((2, parts)),
            dma((2, 3 * parts, xn)),
            dma((2, zn * parts)),
            dma((2, 3 * parts, xn)),
            dma((2, zn)),
            dma((2, xn)),
            dma((2, yn)),
            dma((2, yn)),
            dma((2, yn)),
            dma((2, yn)),
            dma((2, xn)),
            dma((2, zn)),
            dma((7 + parts,)),
        ],
        compiler_params=pltpu.CompilerParams(
            collective_id=0, has_side_effects=True, vmem_limit_bytes=63 * 1024 * 1024
        ),
    )(features, cotangent, w_self, w_neigh, bias.reshape(1, width), neighbours.T, send_rows.reshape(peers, slots).T, hub_local)


def solution(mesh):
    rows = P(("group", "dom"), None)
    return jax.shard_map(
        body,
        mesh=mesh,
        in_specs=(rows, rows, P(), P(), P(), rows, P(("group", "dom"), None, None), P(("group", "dom"))),
        out_specs=(rows, rows),
        check_vma=False,
    )
```

```python
import functools

import jax
import jax.numpy as jnp
from jax import lax
from jax.experimental import pallas as pl
from jax.experimental.pallas import tpu as pltpu
from jax.sharding import PartitionSpec as P

ZN = 12
PARTS = 2
F32 = jnp.float32
BF16 = jnp.bfloat16


def dot(left, right):
    return jnp.dot(left, right, preferred_element_type=F32)


def kernel(
    yn, xn, zn, feat_in, cot_in, ws_in, wn_in, bias_in, nbrt_in, sr_in, hubl, out, gout,
    feat, cot, ws, wn, bias, nbrt, sr, lst, gm,
    tab, tabn, selt, wnt, wst, sel, sel_b, rel, lists, zrows, xsend, bsend, arr, gsend, gback, gback_b, zout, zin, hubtab,
    ha_s, ha, hb_s, hb, hubg, sib_s, sib, yg_s, yg, xb_s, xb, za_s, za,
    sem_z, sem_rz, sem_l, sem_x, sem_b, sem_xg, sem_gb, sem_ha, sem_hb, sem_y, sem_sib, sem_sibg, sem_yg, sem_xb, sem_za, sem_in,
):
    verts, width = feat.shape
    fanout = nbrt.shape[0]
    slots = arr.shape[3]
    lanes = 128
    tall = xn * slots
    quarter = width // lanes
    near = zn * tall
    hub_at = verts + near
    group = lax.axis_index("group")
    dom = lax.axis_index("dom")
    y, core = group // 2, lax.rem(group, 2)
    x, z = dom // zn, lax.rem(dom, zn)
    half_z = zn // 2
    hops = half_z - 2
    parts = sem_z.shape[3]
    cut = width // parts

    def up_y(step):
        return lax.rem(y + step + 2 * yn, yn)

    def up_z(step):
        return lax.rem(z + step + 2 * zn, zn)

    def copy(src, dst, sems, at, **to):
        return pltpu.make_async_remote_copy(
            src_ref=src, dst_ref=dst, send_sem=sems.at[(0,) + at], recv_sem=sems.at[(1,) + at],
            device_id=to, device_id_type=pl.DeviceIdType.MESH,
        )

    def loop(lo, hi, body):
        lax.fori_loop(lo, hi, lambda i, c: (body(i), c)[1], 0)

    z_next = {1: {"dom": x * zn + up_z(1)}, -1: {"dom": x * zn + up_z(-1)}}
    sibling = {"group": y * 2 + 1 - core}

    barrier = pltpu.get_barrier_semaphore()

    def greet(**to):
        pl.semaphore_signal(barrier, 1, device_id=to, device_id_type=pl.DeviceIdType.MESH)

    loop(1, zn, lambda i: greet(dom=x * zn + up_z(i)))
    for i in range(1, xn):
        greet(dom=lax.rem(x + i, xn) * zn + z)
        for step in (-2, -1, 1, 2):
            greet(dom=lax.rem(x + i, xn) * zn + up_z(step))
    for step in (-2, -1, 1, 2):
        greet(group=up_y(step) * 2 + core)
    greet(**sibling)

    sources = (feat_in, sr_in, nbrt_in, cot_in, ws_in, wn_in, bias_in)
    loads = [
        pltpu.make_async_copy(src, dst, sem_in.at[i])
        for i, (src, dst) in enumerate(zip(sources, (feat, sr, nbrt, cot, ws, wn, bias)))
    ]
    for part in range(parts):
        cols = feat_in.at[:, pl.ds(part * cut, cut)]
        loads.append(pltpu.make_async_copy(cols, zrows.at[z, part], sem_in.at[7 + part]))
    for i in (0, 1, 7, 2, 3, 4, 5, 6):
        loads[i].start()
    for load in loads[8:]:
        load.start()
    loads[0].wait()

    row_id = lax.broadcasted_iota(jnp.int32, (16, verts), 0)
    vert_id = lax.broadcasted_iota(jnp.int32, (16, verts), 1)
    hub0, hub1 = hubl[0], hubl[1]
    wanted = jnp.where(row_id == 0, hub0, jnp.where(row_id == 1, hub1, -1))
    hub_rows = dot((vert_id == wanted).astype(BF16), feat[...])
    for q in range(quarter):
        ha_s[2 * q:2 * q + 2, :] = hub_rows[0:2, q * lanes:(q + 1) * lanes]
    ha[z] = ha_s[...]
    loads[1].wait()
    by_peer = sr[...].astype(F32).T
    for xx in range(xn):
        lst[:, xx * slots:(xx + 1) * slots] = by_peer[xx * zn:(xx + 1) * zn, :]
    rel[...] = jnp.full_like(rel, -1.0)
    for d in range(zn):
        rel[d:d + 1, :] = lst[pl.ds(up_z(d), 1), :]
    lists[z] = rel[...].astype(BF16)

    def tally(i):
        sub = lax.broadcasted_iota(jnp.int32, (tall, verts), 0)
        at = i * tall
        zz = i - verts // tall
        border = verts + zz * slots + (sub // slots) * (zn * slots) + lax.rem(sub, slots)
        is_border = jnp.logical_and(zz >= 0, zz < zn)
        rows = jnp.where(is_border, border, at + sub)
        total = jnp.zeros((tall, verts), F32)
        for e in range(fanout):
            total = jnp.where(nbrt[e:e + 1, :] == rows, total + 1.0, total)
        tab[pl.ds(pl.multiple_of(at, tall), tall), :] = total.astype(BF16)
        tabn[i] = total.T.astype(BF16)

    tiles = tab.shape[0] // tall
    spots = 2 * hops + 1
    cuts = [tiles * k // spots for k in range(spots + 1)]

    def tally_part(k):
        loop(cuts[k], cuts[k + 1], tally)

    loads[2].wait()
    tally_part(0)
    for load in loads[7:]:
        load.wait()
    pl.semaphore_wait(barrier, zn - 1 + 5 * (xn - 1) + 5)

    def send_z(way, hop, part):
        piece = zrows.at[up_z(way * (1 - hop)), part]
        return copy(piece, piece, sem_z, (way + 1, hop, part), **z_next[way])

    turns = [(way, part) for part in range(parts) for way in (1, -1)]

    def send_ha(i):
        to = up_z(i)
        return copy(ha_s, ha.at[z], sem_ha, (i,), dom=x * zn + to)

    def send_l(way, hop):
        owner = lists.at[up_z(way * (1 - hop))]
        return copy(owner, owner, sem_l, (way + 1, hop), **z_next[way])

    loop(1, zn, lambda i: send_ha(i).start())
    send_l(1, 1).start()
    send_l(-1, 1).start()
    for way, part in turns:
        send_z(way, 1, part).start()

    sub_id = lax.broadcasted_iota(jnp.int32, (verts, tall), 0).astype(F32)

    def wanted_by(owner, d, sel_at, row):
        chosen = (sub_id == lists[owner, d % zn:d % zn + 1, :].astype(F32)).astype(F32)
        sel_at[...] = chosen.astype(BF16)
        selt[row] = chosen.T.astype(BF16)

    def prepare(way, hop):
        side, owner = (way + 1) // 2, up_z(-way * hop)
        wanted_by(owner, way * hop, sel.at[owner], 3 * side)
        if hop == hops:
            for step in (1, 2):
                wanted_by(owner, way * (hop + step), sel_b.at[side, step - 1], 3 * side + step)

    def pick(way, hop, part):
        side, zz = (way + 1) // 2, up_z(-way * hop)
        if hop == hops:
            rows = dot(selt[3 * side:3 * side + 3].reshape(3 * tall, verts), zrows[zz, part]).astype(BF16)
            for step in (1, 2):
                bsend[side, step - 1, part] = rows[step * tall:(step + 1) * tall].reshape(xn, slots, cut)
                send_beyond(way, step, part)
            rows = rows[:tall]
        else:
            rows = dot(selt[3 * side], zrows[zz, part]).astype(BF16)
        xsend[zz, part] = rows.reshape(xn, slots, cut)
        arr[part, zz, x] = xsend[zz, part, x]
        for i in range(1, xn):
            to = lax.rem(x + i, xn)
            copy(xsend.at[zz, part, to], arr.at[part, zz, x], sem_x, (part,), dom=to * zn + z).start()

    def far_of(way):
        return range(xn // 2) if way > 0 else range(xn // 2, xn)

    def b_slot(way, step):
        return (way + 1) // 2 if step == 1 else 2

    def send_beyond(way, step, part):
        side, slot = (way + 1) // 2, 3 * part + b_slot(way, step)
        for to in range(xn) if step == 1 else far_of(way):
            pltpu.make_async_remote_copy(
                src_ref=bsend.at[side, step - 1, part, to], dst_ref=arr.at[part, up_z(-way * hops), x],
                send_sem=sem_b.at[0, slot, to], recv_sem=sem_b.at[1, slot, x],
                device_id={"dom": to * zn + up_z(way * step)}, device_id_type=pl.DeviceIdType.MESH,
            ).start()

    def hub_z():
        loop(1, zn, lambda i: send_ha(i).wait())
        for zz in range(zn):
            for q in range(quarter):
                hb_s[2 * zz:2 * zz + 2, q * lanes:(q + 1) * lanes] = ha[zz, 2 * q:2 * q + 2, :]
        hb[x] = hb_s[...]
        for i in range(1, xn):
            send_hb(i).start()

    def send_hb(i):
        return copy(hb_s, hb.at[x], sem_hb, (i,), dom=lax.rem(x + i, xn) * zn + z)

    block = hubtab.shape[1]

    lower, upper = pl.ds(0, block // 2), pl.ds(block // 2, block // 2)

    def y_peer(step):
        return {"group": up_y(step) * 2 + core}

    def send_y(i):
        if abs(i) in (1, 2):
            owner, to = y, i
        else:
            owner, to = (up_y(2), -(i == -3) or -2) if i <= 0 else (up_y(-2), i - 2)
        piece = hubtab.at[owner * 2 + core]
        if i in (0, 4):
            piece = piece.at[upper if i == 0 else lower]
        return copy(piece, piece, sem_y, (i % yn,), **y_peer(to))

    def send_sib(i):
        part = hubtab.at[up_y(-i) * 2 + core]
        return copy(part, part, sem_sib, (i,), **sibling)

    def hub_x():
        for i in range(1, xn):
            send_hb(i).wait()
        hubtab[group] = hb[...].reshape(block, width).astype(BF16)
        for i in (2, -2, 1, -1):
            send_y(i).start()
        send_sib(0).start()

    def hub_y():
        send_y(2).wait_recv()
        send_y(3).start()
        send_y(4).start()
        send_y(-2).wait_recv()
        send_y(-3).start()
        send_y(0).start()
        for i in (2, yn - 2):
            send_sib(i).start()
        for i in (1, -1):
            send_y(i).wait_recv()
            send_sib(i % yn).start()

    def hub_end():
        for i in (3, -3, 4):
            send_y(i).wait_recv()
            if i == 4:
                send_y(0).wait_recv()
            send_sib(i % yn).start()

    last = 2 * hops - 1
    hub_steps = [(min(1, last), hub_z), (min(3, last), hub_x), (max(last - 1, 1), hub_y)]
    prepare(1, 0)
    for part in range(parts):
        pick(1, 0, part)
    spot = 0
    for hop in range(1, hops + 1):
        for way in (1, -1):
            send_l(way, hop).wait_recv()
            if hop < hops:
                send_l(way, hop + 1).start()
            prepare(way, hop)
        for part in range(parts):
            for way in (1, -1):
                send_z(way, hop, part).wait_recv()
                if hop < hops:
                    send_z(way, hop + 1, part).start()
                else:
                    pick(way, hop, part)
            if hop < hops:
                pick(1, hop, part)
                pick(-1, hop, part)
            if part in (parts // 2 - 1, parts - 1) and spot < last:
                for at, step in hub_steps:
                    if at == spot:
                        step()
                spot += 1
                tally_part(spot)
    for at, step in hub_steps:
        if at == spot:
            step()
    tally_part(spot + 1)
    hub_end()

    def counts(lo, hi):
        return jnp.concatenate([tabn[i] for i in range(lo // tall, hi // tall)], axis=1)

    for load in loads[3:7]:
        load.wait()
    wnt[...] = wn[...].T
    wst[...] = ws[...].T
    agg = dot(counts(0, verts), feat[...])
    pre = dot(feat[...], ws[...]) + bias[...]
    for i in range(yn):
        send_sib(i).wait()
    agg += dot(counts(hub_at, tab.shape[0]), hubtab[...].reshape(2 * yn * block, width))
    for part in range(parts):
        cols = slice(part * cut, (part + 1) * cut)
        if xn > 1:
            most = (pl.ds(0, 2 * hops + 1), pl.ds(0, xn - 1))
            whole = arr.at[part].at[most]
            copy(whole, whole, sem_x, (part,), dom=lax.rem(x + 1, xn) * zn + z).wait()
        for slot in range(3):
            for i in range(xn):
                copy(bsend.at[0, 0, part, 0], arr.at[part, 0, i], sem_b, (3 * part + slot, i), **sibling).wait()
        summed = agg[:, cols] + dot(counts(verts, hub_at), arr[part].reshape(near, cut))
        pre += dot((summed / fanout).astype(BF16), wn[cols, :])
    sigm = jax.nn.sigmoid(pre)
    grad_pre = (cot[...].astype(F32) * sigm * (1.0 + pre * (1.0 - sigm))).astype(BF16)
    grad_mean = (dot(grad_pre, wnt[...]) / fanout).astype(BF16)
    for part in range(parts):
        gm[part] = grad_mean[:, part * cut:(part + 1) * cut]
    out[...] = (pre * sigm).astype(BF16)

    def slot_grads(zz, part):
        rows = pl.ds(pl.multiple_of(verts + zz * tall, tall), tall)
        gsend[zz, part] = dot(tab[rows, :], gm[part]).astype(BF16).reshape(xn, slots, cut)

    def give_beyond(side, step, slot, to, part):
        way = 2 * side - 1
        return pltpu.make_async_remote_copy(
            src_ref=gsend.at[up_z(-way * (hops + step)), part, to], dst_ref=gback_b.at[side, step - 1, part, x],
            send_sem=sem_gb.at[0, 3 * part + slot, to], recv_sem=sem_gb.at[1, 3 * part + slot, x],
            device_id={"dom": to * zn + up_z(-way * step)}, device_id_type=pl.DeviceIdType.MESH,
        )

    my_side = 1 - x // (xn // 2)
    beyond = [(my_side, 2, 2), (1, 1, 1), (0, 1, 0)]

    def give(j, part):
        zz = up_z(j)
        slot_grads(zz, part)
        gback[zz, part, x] = gsend[zz, part, x]
        for i in range(1, xn):
            to = lax.rem(x + i, xn)
            copy(gsend.at[zz, part, to], gback.at[zz, part, x], sem_xg, (j * parts + part,), dom=to * zn + z).start()

    def give_first(part):
        for side, step, slot in beyond:
            slot_grads(up_z((1 - 2 * side) * (hops + step)), part)
            for to in range(xn):
                give_beyond(side, step, slot, to, part).start()
        give(hops, part)
        give(zn - hops, part)

    give_first(0)
    gback_b[1, 1, :, xn // 2:] = jnp.zeros((parts, xn // 2, slots, cut), BF16)
    gback_b[0, 1, :, :xn // 2] = jnp.zeros((parts, xn // 2, slots, cut), BF16)

    def send_sibg(owner):
        return copy(sib_s.at[owner], sib.at[owner], sem_sibg, (owner,), **sibling)

    def hub_terms(owner):
        rows = pl.ds(pl.multiple_of(hub_at + owner * 2 * block, 32), 2 * block)
        hubg[pl.ds(2 * owner, 2)] = dot(tab[rows, :], grad_mean).reshape(2, block, width)
        sib_s[owner] = hubg[2 * owner + 1 - core].astype(BF16)
        send_sibg(owner).start()

    loop(0, yn, hub_terms)

    for part in range(1, parts):
        give_first(part)

    def give_rest(t):
        j = lax.rem(jnp.where(lax.rem(t, 2) == 1, half_z - (t + 1) // 2, t // 2 - half_z) + zn, zn)
        for part in range(parts):
            give(j, part)

    loop(5, zn, give_rest)

    def given(j, part):
        some = pl.ds(0, xn - 1)
        zz = up_z(j)
        at = (j % zn) * parts + part
        return copy(gsend.at[zz, part, some], gback.at[zz, part, some], sem_xg, (at,), dom=lax.rem(x + 1, xn) * zn + z)

    def owed(j, part):
        if xn > 1:
            given(j, part).wait_recv()
        zz = up_z(j)
        value = dot(sel[zz], gback[zz, part].reshape(tall, cut))
        if abs(j) == hops:
            way = 1 if j < 0 else -1
            side = (way + 1) // 2
            for step in (1, 2):
                slot = 3 * part + b_slot(way, step)
                for i in range(xn) if step == 1 else far_of(way):
                    copy(gsend.at[0, part, 0], gback_b.at[side, step - 1, part, i], sem_gb, (slot, i), **sibling).wait_recv()
                value += dot(sel_b[side, step - 1], gback_b[side, step - 1, part].reshape(tall, cut))
        return value

    def send_g(way, hop, part):
        at = ((way + 1) // 2, hop, part)
        return copy(zout.at[at], zin.at[at], sem_rz, (way + 1, hop, part), **z_next[way])

    def step_z(hop, part):
        for way in (1, -1):
            at = (way + 1) // 2
            value = owed(way * hop, part)
            if hop < hops:
                send_g(way, hop + 1, part).wait_recv()
                value = value + zin[at, hop + 1, part].astype(F32)
            zout[at, hop, part] = value.astype(BF16)
            send_g(way, hop, part).start()

    def mine(owner):
        return hubg[owner * 2 + core] + sib[owner].astype(F32)

    reach = (1, -1, 2, -2, 1, -1, 2, -2)

    def send_yg(i):
        src, dst = yg_s.at[i], yg.at[i]
        if i in (2, 3):
            rows = lower if i == 2 else upper
            src, dst = src.at[rows], dst.at[rows]
        return copy(src, dst, sem_yg, (i,), **y_peer(reach[i]))

    def start_y():
        loop(0, yn, lambda i: send_sibg(i).wait_recv())
        for i, owner in enumerate((3, -3, 4, -4, 1, -1)):
            yg_s[i] = mine(up_y(owner)).astype(BF16)
            send_yg(i).start()

    def relay_y():
        for i in (0, 1):
            send_yg(i).wait_recv()
            send_yg(i + 2).wait_recv()
            value = mine(up_y(reach[i + 6])) + yg[i].astype(F32)
            for at, some in ((0, slice(0, block // 2)), (1, slice(block // 2, block))):
                term = value[some]
                if at == i:
                    term = term + yg[i + 2, some].astype(F32)
                yg_s[i + 6, some] = term.astype(BF16)
            send_yg(i + 6).start()

    def send_xb(i):
        to = lax.rem(x + i, xn)
        return copy(xb_s.at[to], xb.at[i], sem_xb, (i,), dom=to * zn + z)

    def send_za(i):
        to = up_z(i)
        return copy(za_s.at[to], za.at[i], sem_za, (i,), dom=x * zn + to)

    def start_x():
        total = mine(y)
        for i in range(4, 8):
            send_yg(i).wait_recv()
            total = total + yg[i].astype(F32)
        xb_s[...] = total.reshape(xn, 2 * zn, width)
        for i in range(1, xn):
            send_xb(i).start()

    def end_x():
        total = xb_s[x]
        for i in range(1, xn):
            send_xb(i).wait_recv()
            total = total + xb[i]
        for zz in range(zn):
            for q in range(quarter):
                za_s[zz, 2 * q:2 * q + 2, :] = total[2 * zz:2 * zz + 2, q * lanes:(q + 1) * lanes]
        loop(1, zn, lambda i: send_za(i).start())

    def self_part():
        gout[...] = dot(tab[0:verts, :], grad_mean) + dot(grad_pre, wst[...])

    def wait_sent():
        for hop in range(1, hops + 1):
            for way, part in turns:
                send_z(way, hop, part).wait_send()
            send_l(1, hop).wait_send()
            send_l(-1, hop).wait_send()
        for i in (1, -1, 2, -2, 3, -3, 4, 0):
            send_y(i).wait_send()

    def wait_given():
        for hop in range(2, hops + 1):
            for way, part in turns:
                send_g(way, hop, part).wait_send()
        for i in range(8):
            send_yg(i).wait_send()
        for i in range(yn):
            send_sibg(i).wait_send()
        for part in range(parts):
            if xn > 1:
                for j in range(zn):
                    if min(j, zn - j) <= hops:
                        given(j, part).wait_send()
            for side, step, slot in beyond:
                for to in range(xn):
                    give_beyond(side, step, slot, to, part).wait_send()

    end = parts - 1
    jobs = [
        (hops, 0, self_part), (hops, end, wait_sent), (hops - 1, 0, relay_y),
        (min(2, hops), 0, start_x) if hops > 1 else (1, end, start_x),
        (2, end, end_x) if hops > 1 else (1, end, end_x), (1, end, wait_given),
    ]
    start_y()
    for hop in range(hops, 0, -1):
        for part in range(parts):
            step_z(hop, part)
            for at, when, job in jobs:
                if (at, when) == (hop, part):
                    job()
    for part in range(parts):
        cols = slice(part * cut, (part + 1) * cut)
        gout[:, cols] += owed(0, part)
    for way, part in turns:
        cols = slice(part * cut, (part + 1) * cut)
        send_g(way, 1, part).wait_recv()
        gout[:, cols] += zin[(way + 1) // 2, 1, part].astype(F32)
    loop(1, zn, lambda i: send_za(i).wait_recv())
    hub_sum = za_s[z]
    for i in range(1, zn):
        hub_sum = hub_sum + za[i]
    rows_of = lax.broadcasted_iota(jnp.int32, (verts, lanes), 0)
    for q in range(quarter):
        cols = slice(q * lanes, (q + 1) * lanes)
        gout[:, cols] += jnp.where(rows_of == hub0, hub_sum[2 * q:2 * q + 1], 0.0) + jnp.where(
            rows_of == hub1, hub_sum[2 * q + 1:2 * q + 2], 0.0
        )

    for way, part in turns:
        send_g(way, 1, part).wait_send()
    for i in range(1, xn):
        send_xb(i).wait_send()
    loop(1, zn, lambda i: send_za(i).wait_send())


def body(features, cotangent, w_self, w_neigh, bias, neighbours, send_rows, hub_local):
    verts, width = features.shape
    peers, slots = send_rows.shape[1:]
    xn, zn = peers // ZN, ZN
    groups = lax.axis_size("group")
    yn = groups // 2
    half_z, parts = zn // 2, PARTS
    near = peers * slots
    tall = xn * slots
    block = 2 * peers
    tile = width // 64
    cut = width // parts
    vmem = pl.BlockSpec(memory_space=pltpu.VMEM)
    dma = pltpu.SemaphoreType.DMA
    edge = (zn, parts, xn, slots, cut)
    hub = (yn, block, width)
    return pl.pallas_call(
        functools.partial(kernel, yn, xn, zn),
        out_shape=(
            pltpu.VMEM((verts, width), BF16),
            pltpu.VMEM((verts, width), F32),
        ),
        in_specs=[pl.BlockSpec(memory_space=pl.ANY)] * 7 + [pl.BlockSpec(memory_space=pltpu.SMEM)],
        out_specs=(vmem, vmem),
        scratch_shapes=[
            pltpu.VMEM((verts, width), BF16),
            pltpu.VMEM((verts, width), BF16),
            pltpu.VMEM((width, width), BF16),
            pltpu.VMEM((width, width), BF16),
            pltpu.VMEM((1, width), F32),
            pltpu.VMEM(neighbours.shape[::-1], jnp.int32),
            pltpu.VMEM((slots, peers), jnp.int32),
            pltpu.VMEM((zn, tall), F32),
            pltpu.VMEM((parts, verts, cut), BF16),
            pltpu.VMEM((verts + near + groups * block, verts), BF16),
            pltpu.VMEM(((verts + near + groups * block) // tall, verts, tall), BF16),
            pltpu.VMEM((6, tall, verts), BF16),
            pltpu.VMEM((width, width), BF16),
            pltpu.VMEM((width, width), BF16),
            pltpu.VMEM((zn, verts, tall), BF16),
            pltpu.VMEM((2, 2, verts, tall), BF16),
            pltpu.VMEM((16, tall), F32),
            pltpu.VMEM((zn, 16, tall), BF16),
            pltpu.VMEM((zn, parts, verts, cut), BF16),
            pltpu.VMEM(edge, BF16),
            pltpu.VMEM((2, 2) + edge[1:], BF16),
            pltpu.VMEM((parts, zn, xn, slots, cut), BF16),
            pltpu.VMEM(edge, BF16),
            pltpu.VMEM(edge, BF16),
            pltpu.VMEM((2, 2) + edge[1:], BF16),
            pltpu.VMEM((2, half_z - 1, parts, verts, cut), BF16),
            pltpu.VMEM((2, half_z - 1, parts, verts, cut), BF16),
            pltpu.VMEM((groups, block, width), BF16),
            pltpu.VMEM((tile, 128), F32),
            pltpu.VMEM((zn, tile, 128), F32),
            pltpu.VMEM((2 * zn, width), F32),
            pltpu.VMEM((xn, 2 * zn, width), F32),
            pltpu.VMEM((groups, block, width), F32),
            pltpu.VMEM(hub, BF16),
            pltpu.VMEM(hub, BF16),
            pltpu.VMEM(hub, BF16),
            pltpu.VMEM(hub, BF16),
            pltpu.VMEM((xn, 2 * zn, width), F32),
            pltpu.VMEM((xn, 2 * zn, width), F32),
            pltpu.VMEM((zn, tile, 128), F32),
            pltpu.VMEM((zn, tile, 128), F32),
            dma((2, 3, half_z, parts)),
            dma((2, 3, half_z, parts)),
            dma((2, 3, half_z)),
            dma((2, parts)),
            dma((2, 3 * parts, xn)),
            dma((2, zn * parts)),
            dma((2, 3 * parts, xn)),
            dma((2, zn)),
            dma((2, xn)),
            dma((2, yn)),
            dma((2, yn)),
            dma((2, yn)),
            dma((2, yn)),
            dma((2, xn)),
            dma((2, zn)),
            dma((7 + parts,)),
        ],
        compiler_params=pltpu.CompilerParams(
            collective_id=0, has_side_effects=True, vmem_limit_bytes=63 * 1024 * 1024
        ),
    )(features, cotangent, w_self, w_neigh, bias.reshape(1, width), neighbours.T, send_rows.reshape(peers, slots).T, hub_local)


def solution(mesh):
    rows = P(("group", "dom"), None)
    return jax.shard_map(
        body,
        mesh=mesh,
        in_specs=(rows, rows, P(), P(), P(), rows, P(("group", "dom"), None, None), P(("group", "dom"))),
        out_specs=(rows, rows),
        check_vma=False,
    )
```
